32 devices in a mesh: scene: 2 (over x), tile: 8 (over z, y), date: 2 (over core).
Axes of the slice: x: 2, y: 2, z: 4, core: 2. Of those that a mesh axis runs over, the one named last changes fastest.
Arguments:
- slc_real: bfloat16 [32, 512, 256], P('date', ('scene', 'tile')), parts along dimension 1, may hold values from -4.5 to 4.5
- slc_imag: bfloat16 [32, 512, 256], P('date', ('scene', 'tile')), parts along dimension 1, may hold values from -4.5 to 4.5
- pair_offset: int32 [32, 4], replicated, may hold values from 1 to 5, as said below
- pair_weight: int32 [128, 512, 256], P(None, ('scene', 'tile', 'date')), parts along dimension 1, may hold values from 1 to 255
Outputs:
- increments: float32 [31, 512, 256], P(None, ('scene', 'tile', 'date')), parts along dimension 1
The draws below stay inside these ranges and needn't reach their ends.
There are 2 independent parts, one for each index of `scene`. The reference program is written for one: setup_inputs(seed, part) draws one part's arguments, and reference() takes and returns one part's arrays. A program takes and returns all parts, laid end to end along the dimension named above; an argument that names none is the same for every part. Nothing has to cross between parts.
Inputs may be any that keep to these rules, and one draw needn't show every extreme that they name: `pair_offset`: each row holds 4 different offsets in increasing order; 1 and 5 are in every row.
All inputs are finite; a program needn't handle non-finite values.
Results may differ from the reference program's by a relative error of at most 0.0003.
Values may be sent and summed in bfloat16 or wider, within the bound.
A program may use at most 128 MiB of HBM per device.

```python
import math
import jax
import jax.numpy as jnp
from jax import lax

COLS = 256
K = 4
SPAN = 5
SWEEPS = 8
PASSES = 3
STEPS = 2
DATES = 32
PAIRS = 128
INCR = 31
ROWS = 256


def draw_pair_offset(key, part):
    dropped = jax.random.randint(key, (DATES, 1), 2, SPAN).astype(jnp.int32)
    ladder = jnp.arange(1, K + 1, dtype=jnp.int32)[None, :]
    return (ladder + (ladder >= dropped).astype(jnp.int32)).astype(jnp.int32)


def scene_images(key):
    keys = jax.random.split(jax.random.fold_in(key, 9173), 5)
    shape = (DATES, ROWS, COLS)
    scatter = jax.random.uniform(keys[1], (1, ROWS, COLS), jnp.float32, -math.pi, math.pi)
    amplitude = jnp.exp(jax.random.uniform(keys[0], (1, ROWS, COLS), jnp.float32, 0.0, math.log(3.0)))
    motion = 0.5 * jax.random.truncated_normal(keys[2], -3.0, 3.0, shape, jnp.float32)
    noise_re = 0.4 * jax.random.truncated_normal(keys[3], -3.0, 3.0, shape, jnp.float32)
    noise_im = 0.4 * jax.random.truncated_normal(keys[4], -3.0, 3.0, shape, jnp.float32)
    phase = scatter + jnp.cumsum(motion, axis=0)
    real_part = amplitude * jnp.cos(phase) + noise_re
    imag_part = amplitude * jnp.sin(phase) + noise_im
    return (real_part, imag_part)


def draw_slc_real(key, part):
    return scene_images(key)[0].astype(jnp.bfloat16)


def draw_slc_imag(key, part):
    return scene_images(key)[1].astype(jnp.bfloat16)


def set_ends(drawn, key, least, high):
    place = [jax.random.randint(jax.random.fold_in(key, axis), (), 0, length) for axis, length in enumerate(drawn.shape)]
    widest = drawn.shape.index(max(drawn.shape))
    neighbour = place[:widest] + [(place[widest] + 1) % drawn.shape[widest]] + place[widest + 1:]
    return drawn.at[tuple(place)].set(least).at[tuple(neighbour)].set(high)


def setup_inputs(seed: int = 0, part: int = 0) -> dict:
    streams_of = jax.random.split(jax.random.key(seed), 5)
    part_splits = jax.random.split(jax.random.fold_in(streams_of[4], part), 5)
    slc_real = draw_slc_real(jax.random.fold_in(jax.random.fold_in(streams_of[4], part), 71), part)
    slc_imag = draw_slc_imag(jax.random.fold_in(jax.random.fold_in(streams_of[4], part), 71), part)
    pair_offset = draw_pair_offset(jax.random.fold_in(streams_of[4], 71), part)
    pair_weight = set_ends(jax.random.randint(part_splits[3], (PAIRS, ROWS, COLS), 1, 256), jax.random.fold_in(part_splits[3], 1), 1, 255).astype(jnp.int32)
    return {"slc_real": slc_real, "slc_imag": slc_imag, "pair_offset": pair_offset, "pair_weight": pair_weight}


unwrap_damping = 0.08
column_weight = 0.15
solve_damping = 0.1
residual_scale = 0.3

def from_left(values):
    widths = [(0, 0)] * (values.ndim - 1) + [(1, 0)]
    return jnp.pad(values[..., :-1], widths)

def from_right(values):
    widths = [(0, 0)] * (values.ndim - 1) + [(0, 1)]
    return jnp.pad(values[..., 1:], widths)

def coupling(here_re, here_im, there_re, there_im, weight):
    magnitude = jnp.sqrt((here_re * here_re + here_im * here_im) * (there_re * there_re + there_im * there_im))
    link_value = weight * magnitude / (magnitude + 1.0)
    slope_value = (here_im * there_re - here_re * there_im) / (magnitude + 1.0)
    return (link_value, slope_value)

def box_mean(values):
    row_sum = values[..., :-2, :] + values[..., 1:-1, :] + values[..., 2:, :]
    return (from_left(row_sum) + row_sum + from_right(row_sum)) / 9.0

def cell_terms(smooth_re, smooth_im):
    centre_re = smooth_re[..., 1:-1, :]
    centre_im = smooth_im[..., 1:-1, :]
    link_up, slope_up = coupling(centre_re, centre_im, smooth_re[..., :-2, :], smooth_im[..., :-2, :], 1.0)
    link_down, slope_down = coupling(centre_re, centre_im, smooth_re[..., 2:, :], smooth_im[..., 2:, :], 1.0)
    link_left, slope_left = coupling(centre_re, centre_im, from_left(centre_re), from_left(centre_im), column_weight)
    link_right, slope_right = coupling(centre_re, centre_im, from_right(centre_re), from_right(centre_im), column_weight)
    denominator = link_up + link_down + link_left + link_right + unwrap_damping
    source = link_up * slope_up + link_down * slope_down + link_left * slope_left + link_right * slope_right
    return (link_up, link_down, link_left, link_right, denominator, source)

def relax_once(unwrapped, above, below, stencil):
    link_up, link_down, link_left, link_right, denominator, source = stencil
    summed = source + link_up * above + link_down * below + link_left * from_left(unwrapped) + link_right * from_right(unwrapped)
    return summed / denominator

def pair_tables(pair_offset):
    date_count = pair_offset.shape[0]
    per_date = pair_offset.shape[1]
    first_date = jnp.arange(date_count * per_date, dtype=jnp.int32) // per_date
    second = first_date + pair_offset.reshape(-1)
    validity = (second < date_count).astype(jnp.float32)
    unknown = jnp.arange(date_count - 1, dtype=jnp.int32)
    design = ((unknown[None, :] >= first_date[:, None]) & (unknown[None, :] < second[:, None])).astype(jnp.float32)
    return (validity, design)

def forward(design, values):
    return jnp.dot(design, values, precision=lax.Precision.HIGHEST, preferred_element_type=jnp.float32)

def backward(design, values):
    return jnp.dot(design.T, values, precision=lax.Precision.HIGHEST, preferred_element_type=jnp.float32)

def invert(phases, base_weight, design):
    increments = jnp.zeros((design.shape[1], phases.shape[1]), jnp.float32)
    for pass_index in range(PASSES):
        scaled = (phases - forward(design, increments)) / residual_scale
        weights = base_weight / (1.0 + scaled * scaled)
        diagonal = backward(design, weights) + solve_damping
        for step_index in range(STEPS):
            gradient = backward(design, weights * (phases - forward(design, increments))) - solve_damping * increments
            increments = increments + 1.0 / SPAN * gradient / diagonal
    return increments

def reference(slc_real, slc_imag, pair_offset, pair_weight):
    validity, design = pair_tables(pair_offset)
    date_count = pair_offset.shape[0]

    def unwrap_one(pair_number):
        first_date = pair_number // K
        second = first_date + pair_offset[first_date, pair_number % K]
        kept = validity[pair_number]
        clipped = jnp.minimum(second, date_count - 1).astype(jnp.int32)
        first_re = lax.dynamic_index_in_dim(slc_real, first_date, 0, keepdims=False).astype(jnp.float32)
        first_im = lax.dynamic_index_in_dim(slc_imag, first_date, 0, keepdims=False).astype(jnp.float32)
        second_re = lax.dynamic_index_in_dim(slc_real, clipped, 0, keepdims=False).astype(jnp.float32)
        second_im = lax.dynamic_index_in_dim(slc_imag, clipped, 0, keepdims=False).astype(jnp.float32)
        pair_real = kept * (first_re * second_re + first_im * second_im)
        pair_imag = kept * (first_im * second_re - first_re * second_im)
        smooth_re = box_mean(jnp.pad(pair_real, ((1, 1), (0, 0))))
        smooth_im = box_mean(jnp.pad(pair_imag, ((1, 1), (0, 0))))
        stencil = cell_terms(jnp.pad(smooth_re, ((1, 1), (0, 0))), jnp.pad(smooth_im, ((1, 1), (0, 0))))
        unwrapped = jnp.zeros_like(smooth_re)
        for sweep_index in range(SWEEPS):
            above = jnp.pad(unwrapped[:-1], ((1, 0), (0, 0)))
            below = jnp.pad(unwrapped[1:], ((0, 1), (0, 0)))
            unwrapped = relax_once(unwrapped, above, below, stencil)
        return unwrapped
    phases = lax.map(unwrap_one, jnp.arange(PAIRS, dtype=jnp.int32))
    base_weight = pair_weight.astype(jnp.float32) / 255.0 * validity[:, None, None]
    increments = invert(phases.reshape(PAIRS, -1), base_weight.reshape(PAIRS, -1), design)
    return increments.reshape(INCR, ROWS, COLS)
```

```python
import functools

import jax
import jax.numpy as jnp
from jax import lax
from jax.experimental import pallas as pl
from jax.experimental.pallas import tpu as pltpu
from jax.sharding import PartitionSpec as P

SPAN = 5
SWEEPS = 8
PASSES = 3
STEPS = 2

unwrap_damping = 0.08
column_weight = 0.15
solve_damping = 0.1
residual_scale = 0.3

RIM = SWEEPS + 1
MESH = pl.DeviceIdType.MESH
F32 = jnp.float32
BF16 = jnp.bfloat16


def iota(shape, dim):
    return lax.broadcasted_iota(jnp.int32, shape, dim)


def one_hot(condition):
    return jnp.where(condition, 1.0, 0.0).astype(BF16)


def mm(a, b):
    return jnp.dot(a, b, preferred_element_type=F32)


def rcp(x):
    r = pl.reciprocal(x, approx=True)
    return r * (2.0 - x * r)


def split(x):
    high = x.astype(BF16)
    return high, (x - high.astype(F32)).astype(BF16)


def evens_first(columns):
    half = columns // 2
    new = iota((columns, columns), 1)
    old = jnp.where(new < half, 2 * new, 2 * (new - half) + 1)
    return one_hot(iota((columns, columns), 0) == old)


def exchange_kernel(tiles, re_ref, im_ref, out_ref, send_ref, send_sem, recv_sem):
    dates, tile_rows, columns = re_ref.shape
    shard = tile_rows // 2
    scene = lax.axis_index("scene")
    tile = lax.axis_index("tile")
    date = lax.axis_index("date")
    other = 1 - date
    has_up = tile > 0
    has_down = tile < tiles - 1
    barrier = pltpu.get_barrier_semaphore()

    def signal(to_tile, to_date):
        pl.semaphore_signal(
            barrier, inc=1, device_id=(scene, to_tile, to_date), device_id_type=MESH
        )

    signal(tile, other)

    @pl.when(jnp.logical_and(has_up, date == 0))
    def _():
        signal(tile - 1, 0)
        signal(tile - 1, 1)

    @pl.when(jnp.logical_and(has_down, date == 1))
    def _():
        signal(tile + 1, 0)
        signal(tile + 1, 1)

    order = evens_first(columns)
    count = dates * tile_rows
    new = iota((count, 1), 0)
    old = (new % dates) * tile_rows + new // dates
    rows_first = one_hot(iota((count, count), 1) == old)
    for part, ref in enumerate((re_ref, im_ref)):
        flat = ref[...].reshape(count, columns)
        moved = mm(rows_first, mm(flat, order).astype(BF16)).astype(BF16)
        send_ref[:, :, part * columns : (part + 1) * columns] = moved.reshape(
            tile_rows, dates, columns
        )

    pl.semaphore_wait(barrier, 1 + has_up.astype(jnp.int32) + has_down.astype(jnp.int32))

    span = shard + RIM
    mine = pl.ds(pl.multiple_of(date * dates, dates), dates)
    theirs = pl.ds(pl.multiple_of(other * dates, dates), dates)

    def copy(source, target, to_tile, to_date, send_at, recv_at):
        return pltpu.make_async_remote_copy(
            src_ref=send_ref.at[source],
            dst_ref=out_ref.at[target, mine],
            send_sem=send_sem.at[send_at],
            recv_sem=recv_sem.at[recv_at],
            device_id=(scene, to_tile, to_date),
            device_id_type=MESH,
        )

    up_copy = copy(pl.ds(0, RIM), pl.ds(span, RIM), tile - 1, 1, 0, 1 + date)
    down_copy = copy(
        pl.ds(tile_rows - RIM, RIM), pl.ds(0, RIM), tile + 1, 0, 1, 1 + date
    )
    across = copy(
        pl.ds(other * (tile_rows - span), span),
        pl.ds(date * RIM, span),
        tile,
        other,
        2,
        0,
    )

    @pl.when(has_up)
    def _():
        up_copy.start()

    @pl.when(has_down)
    def _():
        down_copy.start()

    across.start()

    out_ref[pl.ds((1 - date) * RIM, span), mine] = send_ref[
        pl.ds(date * (tile_rows - span), span)
    ]
    beyond = date * span
    missing = jnp.logical_or(
        jnp.logical_and(date == 0, tile == 0),
        jnp.logical_and(date == 1, tile == tiles - 1),
    )

    @pl.when(missing)
    def _():
        out_ref[pl.ds(beyond, RIM)] = jnp.zeros((RIM, 2 * dates, 2 * columns), BF16)

    across.wait_send()

    @pl.when(has_up)
    def _():
        up_copy.wait_send()

    @pl.when(has_down)
    def _():
        down_copy.wait_send()

    across.wait_recv()

    @pl.when(jnp.logical_not(missing))
    def _():
        for sender in range(2):
            pltpu.make_async_remote_copy(
                src_ref=send_ref.at[pl.ds(0, RIM)],
                dst_ref=out_ref.at[pl.ds(0, RIM), mine],
                send_sem=send_sem.at[0],
                recv_sem=recv_sem.at[1 + sender],
                device_id=(scene, tile, other),
                device_id_type=MESH,
            ).wait_recv()


def exchange(slc_real, slc_imag, tiles):
    dates, tile_rows, columns = slc_real.shape
    shape = (tile_rows // 2 + 2 * RIM, 2 * dates, 2 * columns)
    whole = pl.BlockSpec(memory_space=pltpu.VMEM)
    return pl.pallas_call(
        functools.partial(exchange_kernel, tiles),
        out_shape=jax.ShapeDtypeStruct(shape, BF16),
        in_specs=[whole, whole],
        out_specs=whole,
        scratch_shapes=[
            pltpu.VMEM((tile_rows, dates, 2 * columns), BF16),
            pltpu.SemaphoreType.DMA((3,)),
            pltpu.SemaphoreType.DMA((3,)),
        ],
        compiler_params=pltpu.CompilerParams(
            collective_id=0, has_side_effects=True, vmem_limit_bytes=24 << 20
        ),
    )(slc_real, slc_imag)


def unwrap_block(block, pairs, formed, coefs, phases, top, bottom, half):
    lines = formed.shape[0]
    here = pl.ds(pl.multiple_of(block * pairs, pairs), pairs)
    lane = iota((pairs, half), 1)
    not_first = jnp.where(lane > 0, 1.0, 0.0)
    not_last = jnp.where(lane < half - 1, 1.0, 0.0)
    between = not_first * column_weight
    back = lambda x: pltpu.roll(x, 1, 1)
    ahead = lambda x: pltpu.roll(x, half - 1, 1)

    def line(at):
        return [formed[at, here, part * half : (part + 1) * half] for part in range(4)]

    smooth = {}
    upper = {}
    levels = [dict() for _ in range(SWEEPS + 1)]

    def smooth_line(at, rows):
        result = []
        for part in (0, 2):
            even, odd = [rows[0][j] + rows[1][j] + rows[2][j] for j in (part, part + 1)]
            both = even + odd
            left = both + back(odd) * not_first
            right = both + ahead(even) * not_last
            if at == RIM - 1:
                left, right = left * top, right * top
            if at == lines - RIM:
                left, right = left * bottom, right * bottom
            result += [left, right]
        re_e, re_o, im_e, im_o = result
        size = []
        for re, im in ((re_e, im_e), (re_o, im_o)):
            power = re * re + im * im
            size.append(power * lax.rsqrt(jnp.maximum(power, 1e-30)))
        return (re_e, im_e, size[0]), (re_o, im_o, size[1])

    def couple(here_z, there_z, weight):
        product = here_z[2] * there_z[2]
        r = rcp(product + 81.0)
        link = product * r
        if weight is not None:
            link = link * weight
        cross = here_z[1] * there_z[0] - here_z[0] * there_z[1]
        return link, link * r * cross

    def stencil(at):
        even, odd = smooth[at]
        inner, inner_s = couple(even, odd, column_weight)
        outer, outer_s = couple(even, tuple(back(x) for x in odd), between)
        outer_next, outer_next_s = ahead(outer), ahead(outer_s)
        sides = ((outer, inner, outer_s + inner_s), (inner, outer_next, -inner_s - outer_next_s))
        first = []
        for j in range(2):
            up, up_s = upper[at][j]
            down, down_s = upper[at + 1][j]
            left, right, side_s = sides[j]
            scale = rcp(up + down + left + right + unwrap_damping)
            source = (up_s - down_s + side_s) * scale
            for k, value in enumerate((up, down, left, right)):
                coefs[at, 5 * j + k] = value * scale
            coefs[at, 5 * j + 4] = source
            first.append(source)
        return first

    def sweep(at, values):
        above, below = values[at - 1], values[at + 1]
        even, odd = values[at]
        beside = ((back(odd), odd), (even, ahead(even)))
        result = []
        for j in range(2):
            total = coefs[at, 5 * j + 4] + coefs[at, 5 * j] * above[j]
            total = total + coefs[at, 5 * j + 1] * below[j]
            total = total + coefs[at, 5 * j + 2] * beside[j][0]
            total = total + coefs[at, 5 * j + 3] * beside[j][1]
            result.append(total)
        return result

    window = [line(0), line(1)]
    for at in range(1, lines - 1):
        window.append(line(at + 1))
        smooth[at] = smooth_line(at, window)
        window.pop(0)
        if at >= 2:
            upper[at] = [couple(smooth[at][j], smooth[at - 1][j], None) for j in range(2)]
        if at >= 3:
            levels[1][at - 1] = stencil(at - 1)
        for level in range(2, SWEEPS + 1):
            row = at - level
            if 1 + level <= row <= lines - 2 - level:
                levels[level][row] = sweep(row, levels[level - 1])
                if level == SWEEPS:
                    for j in range(2):
                        phases[row - RIM, here, j * half : (j + 1) * half] = levels[level][row][j]


def solve_kernel(
    tiles, images, offsets, weight_hbm, out_hbm, formed, coefs, phases, weights, result, load_sem, save_sem
):
    lines, dates, double = images.shape
    columns = double // 2
    half = columns // 2
    per_date = offsets.shape[1]
    pairs = dates * per_date
    rows = phases.shape[0]
    loads = [
        pltpu.make_async_copy(weight_hbm.at[:, r], weights.at[r], load_sem.at[r])
        for r in range(rows)
    ]
    for load in loads:
        load.start()
    tile = lax.axis_index("tile")
    date = lax.axis_index("date")
    top = jnp.where(jnp.logical_and(tile == 0, date == 0), 0.0, 1.0)
    bottom = jnp.where(jnp.logical_and(tile == tiles - 1, date == 1), 0.0, 1.0)

    first = iota((pairs, 1), 0) // per_date
    first_pick = one_hot(iota((pairs, dates), 1) == first)
    of_date = mm(first_pick, offsets[...].astype(F32).astype(BF16))
    own = iota((pairs, per_date), 1) == iota((pairs, per_date), 0) % per_date
    offset = jnp.sum(jnp.where(own, of_date, 0.0), axis=1, keepdims=True)
    second = first + offset.astype(jnp.int32)
    second_pick = one_hot(iota((pairs, dates), 1) == second)
    valid = jnp.where(second < dates, 1.0 / 255.0, 0.0)

    def form(at, carry):
        image = images[at]
        a = mm(first_pick, image)
        b = mm(second_pick, image)
        a_re, a_im = a[:, :columns], a[:, columns:]
        b_re, b_im = b[:, :columns], b[:, columns:]
        formed[at, :, :columns] = a_re * b_re + a_im * b_im
        formed[at, :, columns:] = a_im * b_re - a_re * b_im
        return carry

    lax.fori_loop(0, lines, form, 0)

    block_pairs = 8

    def unwrap(block, carry):
        unwrap_block(block, block_pairs, formed, coefs, phases, top, bottom, half)
        return carry

    lax.fori_loop(0, pairs // block_pairs, unwrap, 0)

    for load in loads:
        load.wait()

    unknown = iota((pairs, dates), 1)
    covers = (unknown >= first) & (unknown < second) & (unknown < dates - 1)
    design = one_hot(covers)
    unknown_t = iota((dates, pairs), 0)
    first_t = iota((dates, pairs), 1) // per_date
    eye = iota((pairs, pairs), 0) == iota((pairs, pairs), 1)
    second_t = jnp.sum(jnp.where(eye, second.astype(F32), 0.0), axis=0, keepdims=True)
    covers_t = (unknown_t >= first_t) & (unknown_t < second_t.astype(jnp.int32))
    design_t = one_hot(covers_t & (unknown_t < dates - 1))
    design2 = jnp.concatenate([design, design], axis=1)
    design2_t = jnp.concatenate([design_t, design_t], axis=1)
    order = evens_first(columns)
    restore = one_hot(
        iota((columns, columns), 0)
        == (iota((columns, columns), 1) // 2 + (iota((columns, columns), 1) % 2) * half)
    )

    def forward(v):
        return mm(design2, jnp.concatenate(split(v), axis=0))

    def backward(x):
        return mm(design2_t, jnp.concatenate(split(x), axis=0))

    group = 4

    def invert(at, carry):
        lanes = range(group)
        index = [at * group + g for g in lanes]
        y = [phases[i] for i in index]
        base = [mm(weights[i].astype(F32).astype(BF16), order) * valid for i in index]
        v = [None] * group
        for pass_index in range(PASSES):
            left = [y[g] - forward(v[g]) if pass_index else y[g] for g in lanes]
            w = [
                base[g] * rcp(1.0 + left[g] * left[g] * (1.0 / residual_scale**2))
                for g in lanes
            ]
            scale = [
                (1.0 / SPAN) * rcp(backward(w[g]) + solve_damping) for g in lanes
            ]
            for step_index in range(STEPS):
                if step_index:
                    left = [y[g] - forward(v[g]) for g in lanes]
                gradient = [backward(w[g] * left[g]) for g in lanes]
                for g in lanes:
                    if v[g] is None:
                        v[g] = gradient[g] * scale[g]
                    else:
                        v[g] = v[g] + (gradient[g] - solve_damping * v[g]) * scale[g]
        for g in lanes:
            high, rest = split(v[g])
            middle, low = split(v[g] - high.astype(F32))
            full = mm(high, restore) + (mm(middle, restore) + mm(low, restore))
            result[index[g]] = full[: dates - 1]
        return carry

    lax.fori_loop(0, rows // group, invert, 0)
    saves = [
        pltpu.make_async_copy(result.at[r], out_hbm.at[:, r], save_sem.at[r])
        for r in range(rows)
    ]
    for save in saves:
        save.start()
    for save in saves:
        save.wait()


def solve(images, pair_offset, pair_weight, tiles):
    lines, dates, double = images.shape
    columns = double // 2
    pairs, rows = pair_weight.shape[:2]
    whole = pl.BlockSpec(memory_space=pltpu.VMEM)
    return pl.pallas_call(
        functools.partial(solve_kernel, tiles),
        out_shape=jax.ShapeDtypeStruct((dates - 1, rows, columns), F32),
        in_specs=[whole, whole, pl.BlockSpec(memory_space=pl.ANY)],
        out_specs=pl.BlockSpec(memory_space=pl.ANY),
        scratch_shapes=[
            pltpu.VMEM((lines, pairs, double), F32),
            pltpu.VMEM((lines, 10, 8, columns // 2), F32),
            pltpu.VMEM((rows, pairs, columns), F32),
            pltpu.VMEM((rows, pairs, columns), jnp.int32),
            pltpu.VMEM((rows, dates - 1, columns), F32),
            pltpu.SemaphoreType.DMA((rows,)),
            pltpu.SemaphoreType.DMA((rows,)),
        ],
        compiler_params=pltpu.CompilerParams(vmem_limit_bytes=40 << 20),
    )(images, pair_offset, pair_weight)


def local(slc_real, slc_imag, pair_offset, pair_weight, tiles):
    images = exchange(slc_real, slc_imag, tiles)
    return solve(images, pair_offset, pair_weight, tiles)


def solution(mesh):
    placed = (
        P("date", ("scene", "tile"), None),
        P("date", ("scene", "tile"), None),
        P(),
        P(None, ("scene", "tile", "date"), None),
    )
    return jax.shard_map(
        functools.partial(local, tiles=mesh.shape["tile"]),
        mesh=mesh,
        in_specs=placed,
        out_specs=P(None, ("scene", "tile", "date"), None),
        check_vma=False,
    )
```

```python
import functools

import jax
import jax.numpy as jnp
from jax import lax
from jax.experimental import pallas as pl
from jax.experimental.pallas import tpu as pltpu
from jax.sharding import PartitionSpec as P

SPAN = 5
SWEEPS = 8
PASSES = 3
STEPS = 2

unwrap_damping = 0.08
column_weight = 0.15
solve_damping = 0.1
residual_scale = 0.3

RIM = SWEEPS + 1
MESH = pl.DeviceIdType.MESH
F32 = jnp.float32
BF16 = jnp.bfloat16


def iota(shape, dim):
    return lax.broadcasted_iota(jnp.int32, shape, dim)


def one_hot(condition):
    return jnp.where(condition, 1.0, 0.0).astype(BF16)


def mm(a, b):
    return jnp.dot(a, b, preferred_element_type=F32)


def rcp(x):
    return pl.reciprocal(x, approx=True)


def split(x):
    high = x.astype(BF16)
    return high, (x - high.astype(F32)).astype(BF16)


def evens_first(columns):
    half = columns // 2
    new = iota((columns, columns), 1)
    old = jnp.where(new < half, 2 * new, 2 * (new - half) + 1)
    return one_hot(iota((columns, columns), 0) == old)


def exchange_kernel(
    tiles, re_hbm, im_hbm, out_ref, parts_ref, send_ref, zeros, load_sem, send_sem, recv_sem
):
    dates, tile_rows, columns = re_hbm.shape
    loads = [
        pltpu.make_async_copy(hbm, parts_ref.at[part], load_sem.at[part])
        for part, hbm in enumerate((re_hbm, im_hbm))
    ]
    for load in loads:
        load.start()
    shard = tile_rows // 2
    scene = lax.axis_index("scene")
    tile = lax.axis_index("tile")
    date = lax.axis_index("date")
    other = 1 - date
    has_up = tile > 0
    has_down = tile < tiles - 1
    barrier = pltpu.get_barrier_semaphore()

    def signal(to_tile, to_date):
        pl.semaphore_signal(
            barrier, inc=1, device_id=(scene, to_tile, to_date), device_id_type=MESH
        )

    signal(tile, other)

    @pl.when(jnp.logical_and(has_up, date == 0))
    def _():
        signal(tile - 1, 0)
        signal(tile - 1, 1)

    @pl.when(jnp.logical_and(has_down, date == 1))
    def _():
        signal(tile + 1, 0)
        signal(tile + 1, 1)

    order = evens_first(columns)
    count = dates * tile_rows

    def arrange(start, size):
        new = iota((size * dates, 1), 0) + start * dates
        old = (new % dates) * tile_rows + new // dates
        pick = one_hot(iota((size * dates, count), 1) == old)
        for part in range(2):
            moved = mm(pick, parts_ref[part].reshape(count, columns)).astype(BF16)
            send_ref[start : start + size, :, part * columns : (part + 1) * columns] = (
                mm(moved, order).astype(BF16).reshape(size, dates, columns)
            )

    for load in loads:
        load.wait()
    arrange(0, RIM)
    arrange(tile_rows - RIM, RIM)

    pl.semaphore_wait(barrier, 1 + has_up.astype(jnp.int32) + has_down.astype(jnp.int32))

    span = shard + RIM
    mine = pl.ds(pl.multiple_of(date * dates, dates), dates)

    def copy(source, target, to_tile, to_date, send_at, recv_at):
        return pltpu.make_async_remote_copy(
            src_ref=send_ref.at[source],
            dst_ref=out_ref.at[target, mine],
            send_sem=send_sem.at[send_at],
            recv_sem=recv_sem.at[recv_at],
            device_id=(scene, to_tile, to_date),
            device_id_type=MESH,
        )

    up_copy = copy(pl.ds(0, RIM), pl.ds(span, RIM), tile - 1, 1, 0, 1 + date)
    down_copy = copy(
        pl.ds(tile_rows - RIM, RIM), pl.ds(0, RIM), tile + 1, 0, 1, 1 + date
    )
    across = copy(
        pl.ds(other * (tile_rows - span), span),
        pl.ds(date * RIM, span),
        tile,
        other,
        2,
        0,
    )

    @pl.when(has_up)
    def _():
        up_copy.start()

    @pl.when(has_down)
    def _():
        down_copy.start()

    arrange(RIM, tile_rows - 2 * RIM)
    across.start()

    keep = pltpu.make_async_copy(
        send_ref.at[pl.ds(date * (tile_rows - span), span)],
        out_ref.at[pl.ds((1 - date) * RIM, span), mine],
        load_sem.at[0],
    )
    keep.start()
    missing = jnp.logical_or(
        jnp.logical_and(date == 0, tile == 0),
        jnp.logical_and(date == 1, tile == tiles - 1),
    )

    @pl.when(missing)
    def _():
        zeros[...] = jnp.zeros(zeros.shape, BF16)
        clear = pltpu.make_async_copy(
            zeros, out_ref.at[pl.ds(date * span, RIM)], load_sem.at[1]
        )
        clear.start()
        clear.wait()

    keep.wait()
    across.wait_send()

    @pl.when(has_up)
    def _():
        up_copy.wait_send()

    @pl.when(has_down)
    def _():
        down_copy.wait_send()

    across.wait_recv()

    @pl.when(jnp.logical_not(missing))
    def _():
        for sender in range(2):
            pltpu.make_async_remote_copy(
                src_ref=send_ref.at[pl.ds(0, RIM)],
                dst_ref=out_ref.at[pl.ds(0, RIM), mine],
                send_sem=send_sem.at[0],
                recv_sem=recv_sem.at[1 + sender],
                device_id=(scene, tile, other),
                device_id_type=MESH,
            ).wait_recv()


def exchange(slc_real, slc_imag, tiles):
    dates, tile_rows, columns = slc_real.shape
    shape = (tile_rows // 2 + 2 * RIM, 2 * dates, 2 * columns)
    return pl.pallas_call(
        functools.partial(exchange_kernel, tiles),
        out_shape=jax.ShapeDtypeStruct(shape, BF16),
        in_specs=[pl.BlockSpec(memory_space=pl.ANY)] * 2,
        out_specs=pl.BlockSpec(memory_space=pl.ANY),
        scratch_shapes=[
            pltpu.VMEM((2, dates, tile_rows, columns), BF16),
            pltpu.VMEM((tile_rows, dates, 2 * columns), BF16),
            pltpu.VMEM((RIM, 2 * dates, 2 * columns), BF16),
            pltpu.SemaphoreType.DMA((2,)),
            pltpu.SemaphoreType.DMA((3,)),
            pltpu.SemaphoreType.DMA((3,)),
        ],
        compiler_params=pltpu.CompilerParams(
            collective_id=0, has_side_effects=True, vmem_limit_bytes=(64 << 20) - 1280 * 1024
        ),
    )(slc_real, slc_imag)


def unwrap_block(block, pairs, formed, coefs, phases, top, bottom, half):
    lines = formed.shape[0]
    here = pl.ds(pl.multiple_of(block * pairs, pairs), pairs)
    lane = iota((pairs, half), 1)
    not_first = jnp.where(lane > 0, 1.0, 0.0)
    not_last = jnp.where(lane < half - 1, 1.0, 0.0)
    between = not_first * column_weight
    back = lambda x: pltpu.roll(x, 1, 1)
    ahead = lambda x: pltpu.roll(x, half - 1, 1)

    def line(at):
        return [formed[at, here, part * half : (part + 1) * half] for part in range(4)]

    smooth = {}
    upper = {}
    levels = [dict() for _ in range(SWEEPS + 1)]

    def smooth_line(at, rows):
        result = []
        for part in (0, 2):
            even, odd = [rows[0][j] + rows[1][j] + rows[2][j] for j in (part, part + 1)]
            both = even + odd
            left = both + back(odd) * not_first
            right = both + ahead(even) * not_last
            if at == RIM - 1:
                left, right = left * top, right * top
            if at == lines - RIM:
                left, right = left * bottom, right * bottom
            result += [left, right]
        re_e, re_o, im_e, im_o = result
        size = []
        for re, im in ((re_e, im_e), (re_o, im_o)):
            power = re * re + im * im
            size.append(power * lax.rsqrt(jnp.maximum(power, 1e-30)))
        return (re_e, im_e, size[0]), (re_o, im_o, size[1])

    def couple(here_z, there_z, weight):
        product = here_z[2] * there_z[2]
        r = rcp(product + 81.0)
        link = product * r
        if weight is not None:
            link = link * weight
        cross = here_z[1] * there_z[0] - here_z[0] * there_z[1]
        return link, link * r * cross

    def stencil(at):
        even, odd = smooth[at]
        inner, inner_s = couple(even, odd, column_weight)
        outer, outer_s = couple(even, tuple(back(x) for x in odd), between)
        outer_next, outer_next_s = ahead(outer), ahead(outer_s)
        sides = ((outer, inner, outer_s + inner_s), (inner, outer_next, -inner_s - outer_next_s))
        first = []
        for j in range(2):
            up, up_s = upper[at][j]
            down, down_s = upper[at + 1][j]
            left, right, side_s = sides[j]
            scale = rcp(up + down + left + right + unwrap_damping)
            source = (up_s - down_s + side_s) * scale
            for k, value in enumerate((up, down, left, right)):
                coefs[at, 5 * j + k] = value * scale
            coefs[at, 5 * j + 4] = source
            first.append(source)
        return first

    def sweep(at, values):
        above, below = values[at - 1], values[at + 1]
        even, odd = values[at]
        beside = ((back(odd), odd), (even, ahead(even)))
        result = []
        for j in range(2):
            vertical = coefs[at, 5 * j] * above[j] + coefs[at, 5 * j + 1] * below[j]
            sides = coefs[at, 5 * j + 2] * beside[j][0] + coefs[at, 5 * j + 3] * beside[j][1]
            total = (coefs[at, 5 * j + 4] + vertical) + sides
            result.append(total)
        return result

    window = [line(0), line(1)]
    for step in range(1, lines + SWEEPS):
        for level in range(SWEEPS, 1, -1):
            row = step - 1 - 2 * level
            if 1 + level <= row <= lines - 2 - level:
                values = sweep(row, levels[level - 1])
                levels[level][row] = values
                if level == SWEEPS:
                    for j in range(2):
                        phases[row - RIM, here, j * half : (j + 1) * half] = values[j]
        if 2 <= step - 3 <= lines - 3:
            levels[1][step - 3] = stencil(step - 3)
        if 2 <= step - 1 <= lines - 2:
            upper[step - 1] = [
                couple(smooth[step - 1][j], smooth[step - 2][j], None) for j in range(2)
            ]
        if step <= lines - 2:
            window.append(line(step + 1))
            smooth[step] = smooth_line(step, window)
            window.pop(0)


def solve_kernel(
    tiles, images_hbm, offsets, weight_hbm, out_hbm, images, formed, coefs, phases, weights, result, line_sem, load_sem, save_sem
):
    lines, dates, double = images_hbm.shape
    columns = double // 2
    half = columns // 2
    per_date = offsets.shape[0]
    pairs = dates * per_date
    rows = phases.shape[0]
    chunk = 4
    fetches = [
        pltpu.make_async_copy(
            images_hbm.at[pl.ds(at, min(chunk, lines - at))],
            images.at[pl.ds(at, min(chunk, lines - at))],
            line_sem.at[at // chunk],
        )
        for at in range(0, lines, chunk)
    ]
    for fetch in fetches:
        fetch.start()
    loads = [
        pltpu.make_async_copy(weight_hbm.at[:, r], weights.at[r], load_sem.at[r])
        for r in range(rows)
    ]
    for load in loads:
        load.start()
    tile = lax.axis_index("tile")
    date = lax.axis_index("date")
    top = jnp.where(jnp.logical_and(tile == 0, date == 0), 0.0, 1.0)
    bottom = jnp.where(jnp.logical_and(tile == tiles - 1, date == 1), 0.0, 1.0)

    first = iota((pairs, 1), 0) // per_date
    first_pick = one_hot(iota((pairs, dates), 1) == first)
    of_date = lax.dot_general(
        first_pick,
        offsets[...].astype(F32).astype(BF16),
        (((1,), (1,)), ((), ())),
        preferred_element_type=F32,
    )
    own = iota((pairs, per_date), 1) == iota((pairs, per_date), 0) % per_date
    offset = jnp.sum(jnp.where(own, of_date, 0.0), axis=1, keepdims=True)
    second = first + offset.astype(jnp.int32)
    second_pick = one_hot(iota((pairs, dates), 1) == second)
    valid = jnp.where(second < dates, 1.0 / 255.0, 0.0)

    def form(at):
        image = images[at]
        a = mm(first_pick, image)
        b = mm(second_pick, image)
        a_re, a_im = a[:, :columns], a[:, columns:]
        b_re, b_im = b[:, :columns], b[:, columns:]
        formed[at, :, :columns] = a_re * b_re + a_im * b_im
        formed[at, :, columns:] = a_im * b_re - a_re * b_im

    for at in range(lines):
        if at % chunk == 0:
            fetches[at // chunk].wait()
        form(at)

    block_pairs = 8

    def unwrap(block, carry):
        unwrap_block(block, block_pairs, formed, coefs, phases, top, bottom, half)
        return carry

    lax.fori_loop(0, pairs // block_pairs, unwrap, 0)

    for load in loads:
        load.wait()

    unknown = iota((pairs, dates), 1)
    covers = (unknown >= first) & (unknown < second) & (unknown < dates - 1)
    design = one_hot(covers)
    unknown_t = iota((dates, pairs), 0)
    first_t = iota((dates, pairs), 1) // per_date
    eye = iota((pairs, pairs), 0) == iota((pairs, pairs), 1)
    second_t = jnp.sum(jnp.where(eye, second.astype(F32), 0.0), axis=0, keepdims=True)
    covers_t = (unknown_t >= first_t) & (unknown_t < second_t.astype(jnp.int32))
    design_t = one_hot(covers_t & (unknown_t < dates - 1))
    design2 = jnp.concatenate([design, design], axis=1)
    design2_t = jnp.concatenate([design_t, design_t], axis=1)
    order = evens_first(columns)
    restore = one_hot(
        iota((columns, columns), 0)
        == (iota((columns, columns), 1) // 2 + (iota((columns, columns), 1) % 2) * half)
    )

    def forward(v):
        return mm(design2, jnp.concatenate(split(v), axis=0))

    def backward(x):
        return mm(design2_t, jnp.concatenate(split(x), axis=0))

    group = 8 if rows % 8 == 0 else 1

    def invert(at, carry):
        lanes = range(group)
        index = [at * group + g for g in lanes]
        y = [phases[i] for i in index]
        base = [mm(weights[i].astype(F32).astype(BF16), order) * valid for i in index]
        v = [None] * group
        for pass_index in range(PASSES):
            left = [y[g] - forward(v[g]) if pass_index else y[g] for g in lanes]
            w = [
                base[g] * rcp(1.0 + left[g] * left[g] * (1.0 / residual_scale**2))
                for g in lanes
            ]
            scale = [
                (1.0 / SPAN) * rcp(backward(w[g]) + solve_damping) for g in lanes
            ]
            for step_index in range(STEPS):
                if step_index:
                    left = [y[g] - forward(v[g]) for g in lanes]
                gradient = [backward(w[g] * left[g]) for g in lanes]
                for g in lanes:
                    if v[g] is None:
                        v[g] = gradient[g] * scale[g]
                    else:
                        v[g] = v[g] + (gradient[g] - solve_damping * v[g]) * scale[g]
        for g in lanes:
            high, rest = split(v[g])
            middle, low = split(v[g] - high.astype(F32))
            full = mm(high, restore) + (mm(middle, restore) + mm(low, restore))
            result[index[g]] = full[: dates - 1]
        return carry

    lax.fori_loop(0, rows // group, invert, 0)
    saves = [
        pltpu.make_async_copy(result.at[r], out_hbm.at[:, r], save_sem.at[r])
        for r in range(rows)
    ]
    for save in saves:
        save.start()
    for save in saves:
        save.wait()


def solve(images, pair_offset, pair_weight, tiles):
    lines, dates, double = images.shape
    columns = double // 2
    pairs, rows = pair_weight.shape[:2]
    whole = pl.BlockSpec(memory_space=pltpu.VMEM)
    return pl.pallas_call(
        functools.partial(solve_kernel, tiles),
        out_shape=jax.ShapeDtypeStruct((dates - 1, rows, columns), F32),
        in_specs=[pl.BlockSpec(memory_space=pl.ANY), whole, pl.BlockSpec(memory_space=pl.ANY)],
        out_specs=pl.BlockSpec(memory_space=pl.ANY),
        scratch_shapes=[
            pltpu.VMEM(images.shape, BF16),
            pltpu.VMEM((lines, pairs, double), F32),
            pltpu.VMEM((lines, 10, 8, columns // 2), F32),
            pltpu.VMEM((rows, pairs, columns), F32),
            pltpu.VMEM((rows, pairs, columns), jnp.int32),
            pltpu.VMEM((rows, dates - 1, columns), F32),
            pltpu.SemaphoreType.DMA((lines,)),
            pltpu.SemaphoreType.DMA((rows,)),
            pltpu.SemaphoreType.DMA((rows,)),
        ],
        compiler_params=pltpu.CompilerParams(vmem_limit_bytes=(64 << 20) - 1280 * 1024),
    )(images, pair_offset, pair_weight)


def local(slc_real, slc_imag, pair_offset, pair_weight, tiles):
    images = exchange(slc_real, slc_imag, tiles)
    return solve(images, pair_offset.T, pair_weight, tiles)


def solution(mesh):
    placed = (
        P("date", ("scene", "tile"), None),
        P("date", ("scene", "tile"), None),
        P(),
        P(None, ("scene", "tile", "date"), None),
    )
    return jax.shard_map(
        functools.partial(local, tiles=mesh.shape["tile"]),
        mesh=mesh,
        in_specs=placed,
        out_specs=P(None, ("scene", "tile", "date"), None),
        check_vma=False,
    )
```

```python
import functools

import jax
import jax.numpy as jnp
from jax import lax
from jax.experimental import pallas as pl
from jax.experimental.pallas import tpu as pltpu
from jax.sharding import PartitionSpec as P

SPAN = 5
SWEEPS = 8
PASSES = 3
STEPS = 2

unwrap_damping = 0.08
column_weight = 0.15
solve_damping = 0.1
residual_scale = 0.3

RIM = SWEEPS + 1
MESH = pl.DeviceIdType.MESH
F32 = jnp.float32
BF16 = jnp.bfloat16


def iota(shape, dim):
    return lax.broadcasted_iota(jnp.int32, shape, dim)


def one_hot(condition):
    return jnp.where(condition, 1.0, 0.0).astype(BF16)


def mm(a, b):
    return jnp.dot(a, b, preferred_element_type=F32)


def rcp(x):
    return pl.reciprocal(x, approx=True)


def split(x):
    high = x.astype(BF16)
    return high, (x - high.astype(F32)).astype(BF16)


def evens_first(columns):
    half = columns // 2
    new = iota((columns, columns), 1)
    old = jnp.where(new < half, 2 * new, 2 * (new - half) + 1)
    return one_hot(iota((columns, columns), 0) == old)


def exchange_kernel(
    tiles, re_hbm, im_hbm, out_ref, parts_ref, send_ref, zeros, load_sem, send_sem, recv_sem
):
    dates, tile_rows, columns = re_hbm.shape
    loads = [
        pltpu.make_async_copy(hbm, parts_ref.at[part], load_sem.at[part])
        for part, hbm in enumerate((re_hbm, im_hbm))
    ]
    for load in loads:
        load.start()
    shard = tile_rows // 2
    scene = lax.axis_index("scene")
    tile = lax.axis_index("tile")
    date = lax.axis_index("date")
    other = 1 - date
    has_up = tile > 0
    has_down = tile < tiles - 1
    barrier = pltpu.get_barrier_semaphore()

    def signal(to_tile, to_date):
        pl.semaphore_signal(
            barrier, inc=1, device_id=(scene, to_tile, to_date), device_id_type=MESH
        )

    signal(tile, other)

    @pl.when(jnp.logical_and(has_up, date == 0))
    def _():
        signal(tile - 1, 0)
        signal(tile - 1, 1)

    @pl.when(jnp.logical_and(has_down, date == 1))
    def _():
        signal(tile + 1, 0)
        signal(tile + 1, 1)

    order = evens_first(columns)
    count = dates * tile_rows

    def arrange(start, size):
        new = iota((size * dates, 1), 0) + start * dates
        old = (new % dates) * tile_rows + new // dates
        pick = one_hot(iota((size * dates, count), 1) == old)
        for part in range(2):
            moved = mm(pick, parts_ref[part].reshape(count, columns)).astype(BF16)
            send_ref[start : start + size, :, part * columns : (part + 1) * columns] = (
                mm(moved, order).astype(BF16).reshape(size, dates, columns)
            )

    for load in loads:
        load.wait()
    arrange(0, RIM)
    arrange(tile_rows - RIM, RIM)

    pl.semaphore_wait(barrier, 1 + has_up.astype(jnp.int32) + has_down.astype(jnp.int32))

    span = shard + RIM
    mine = pl.ds(pl.multiple_of(date * dates, dates), dates)

    def copy(source, target, to_tile, to_date, send_at, recv_at):
        return pltpu.make_async_remote_copy(
            src_ref=send_ref.at[source],
            dst_ref=out_ref.at[target, mine],
            send_sem=send_sem.at[send_at],
            recv_sem=recv_sem.at[recv_at],
            device_id=(scene, to_tile, to_date),
            device_id_type=MESH,
        )

    up_copy = copy(pl.ds(0, RIM), pl.ds(span, RIM), tile - 1, 1, 0, 1 + date)
    down_copy = copy(
        pl.ds(tile_rows - RIM, RIM), pl.ds(0, RIM), tile + 1, 0, 1, 1 + date
    )
    across = copy(
        pl.ds(other * (tile_rows - span), span),
        pl.ds(date * RIM, span),
        tile,
        other,
        2,
        0,
    )

    @pl.when(has_up)
    def _():
        up_copy.start()

    @pl.when(has_down)
    def _():
        down_copy.start()

    arrange(RIM, tile_rows - 2 * RIM)
    across.start()

    keep = pltpu.make_async_copy(
        send_ref.at[pl.ds(date * (tile_rows - span), span)],
        out_ref.at[pl.ds((1 - date) * RIM, span), mine],
        load_sem.at[0],
    )
    keep.start()
    missing = jnp.logical_or(
        jnp.logical_and(date == 0, tile == 0),
        jnp.logical_and(date == 1, tile == tiles - 1),
    )

    @pl.when(missing)
    def _():
        zeros[...] = jnp.zeros(zeros.shape, BF16)
        clear = pltpu.make_async_copy(
            zeros, out_ref.at[pl.ds(date * span, RIM)], load_sem.at[1]
        )
        clear.start()
        clear.wait()

    keep.wait()
    across.wait_send()

    @pl.when(has_up)
    def _():
        up_copy.wait_send()

    @pl.when(has_down)
    def _():
        down_copy.wait_send()

    across.wait_recv()

    @pl.when(jnp.logical_not(missing))
    def _():
        for sender in range(2):
            pltpu.make_async_remote_copy(
                src_ref=send_ref.at[pl.ds(0, RIM)],
                dst_ref=out_ref.at[pl.ds(0, RIM), mine],
                send_sem=send_sem.at[0],
                recv_sem=recv_sem.at[1 + sender],
                device_id=(scene, tile, other),
                device_id_type=MESH,
            ).wait_recv()


def exchange(slc_real, slc_imag, tiles):
    dates, tile_rows, columns = slc_real.shape
    shape = (tile_rows // 2 + 2 * RIM, 2 * dates, 2 * columns)
    return pl.pallas_call(
        functools.partial(exchange_kernel, tiles),
        out_shape=jax.ShapeDtypeStruct(shape, BF16),
        in_specs=[pl.BlockSpec(memory_space=pl.ANY)] * 2,
        out_specs=pl.BlockSpec(memory_space=pl.ANY),
        scratch_shapes=[
            pltpu.VMEM((2, dates, tile_rows, columns), BF16),
            pltpu.VMEM((tile_rows, dates, 2 * columns), BF16),
            pltpu.VMEM((RIM, 2 * dates, 2 * columns), BF16),
            pltpu.SemaphoreType.DMA((2,)),
            pltpu.SemaphoreType.DMA((3,)),
            pltpu.SemaphoreType.DMA((3,)),
        ],
        compiler_params=pltpu.CompilerParams(
            collective_id=0, has_side_effects=True, vmem_limit_bytes=(64 << 20) - 1280 * 1024
        ),
    )(slc_real, slc_imag)


def stencil_block(block, pairs, formed, coefs, top, bottom, half):
    lines = formed.shape[0]
    here = pl.ds(pl.multiple_of(block * pairs, pairs), pairs)
    lane = iota((pairs, half), 1)
    not_first = jnp.where(lane > 0, 1.0, 0.0)
    not_last = jnp.where(lane < half - 1, 1.0, 0.0)
    between = not_first * column_weight
    back = lambda x: pltpu.roll(x, 1, 1)
    ahead = lambda x: pltpu.roll(x, half - 1, 1)

    def line(at):
        return [formed[at, here, part * half : (part + 1) * half] for part in range(4)]

    smooth = {}
    upper = {}

    def smooth_line(at, rows):
        result = []
        for part in (0, 2):
            even, odd = [rows[0][j] + rows[1][j] + rows[2][j] for j in (part, part + 1)]
            both = even + odd
            left = both + back(odd) * not_first
            right = both + ahead(even) * not_last
            if at == RIM - 1:
                left, right = left * top, right * top
            if at == lines - RIM:
                left, right = left * bottom, right * bottom
            result += [left, right]
        re_e, re_o, im_e, im_o = result
        size = []
        for re, im in ((re_e, im_e), (re_o, im_o)):
            power = re * re + im * im
            size.append(power * lax.rsqrt(jnp.maximum(power, 1e-30)))
        return (re_e, im_e, size[0]), (re_o, im_o, size[1])

    def couple(here_z, there_z, weight):
        product = here_z[2] * there_z[2]
        r = rcp(product + 81.0)
        link = product * r
        if weight is not None:
            link = link * weight
        cross = here_z[1] * there_z[0] - here_z[0] * there_z[1]
        return link, link * r * cross

    def stencil(at):
        even, odd = smooth[at]
        inner, inner_s = couple(even, odd, column_weight)
        outer, outer_s = couple(even, tuple(back(x) for x in odd), between)
        outer_next, outer_next_s = ahead(outer), ahead(outer_s)
        sides = ((outer, inner, outer_s + inner_s), (inner, outer_next, -inner_s - outer_next_s))
        for j in range(2):
            up, up_s = upper[at][j]
            down, down_s = upper[at + 1][j]
            left, right, side_s = sides[j]
            scale = rcp(up + down + left + right + unwrap_damping)
            source = up_s - down_s + side_s
            for k, value in enumerate((up, down, left, right, source)):
                coefs[at, 5 * j + k, here] = value * scale

    window = [line(0), line(1)]
    for step in range(1, lines + 1):
        if 2 <= step - 3 <= lines - 3:
            stencil(step - 3)
        if 2 <= step - 1 <= lines - 2:
            upper[step - 1] = [
                couple(smooth[step - 1][j], smooth[step - 2][j], None) for j in range(2)
            ]
        if step <= lines - 2:
            window.append(line(step + 1))
            smooth[step] = smooth_line(step, window)
            window.pop(0)


def sweep_block(block, pairs, lines, coefs, phases, half):
    here = pl.ds(pl.multiple_of(block * pairs, pairs), pairs)
    back = lambda x: pltpu.roll(x, 1, 1)
    ahead = lambda x: pltpu.roll(x, half - 1, 1)
    levels = [dict() for _ in range(SWEEPS + 1)]

    def sweep(at, values):
        above, below = values[at - 1], values[at + 1]
        even, odd = values[at]
        beside = ((back(odd), odd), (even, ahead(even)))
        result = []
        for j in range(2):
            vertical = coefs[at, 5 * j, here] * above[j] + coefs[at, 5 * j + 1, here] * below[j]
            sides = coefs[at, 5 * j + 2, here] * beside[j][0] + coefs[at, 5 * j + 3, here] * beside[j][1]
            total = (coefs[at, 5 * j + 4, here] + vertical) + sides
            result.append(total)
        return result

    for step in range(5, lines + SWEEPS):
        for level in range(SWEEPS, 1, -1):
            row = step - 1 - 2 * level
            if 1 + level <= row <= lines - 2 - level:
                values = sweep(row, levels[level - 1])
                levels[level][row] = values
                if level == SWEEPS:
                    for j in range(2):
                        phases[row - RIM, here, j * half : (j + 1) * half] = values[j]
        if 2 <= step - 3 <= lines - 3:
            levels[1][step - 3] = [coefs[step - 3, 5 * j + 4, here] for j in range(2)]


def solve_kernel(
    tiles, images_hbm, offsets, weight_hbm, out_hbm, images, formed, coefs, phases, weights, result, line_sem, load_sem, save_sem
):
    lines, dates, double = images_hbm.shape
    columns = double // 2
    half = columns // 2
    per_date = offsets.shape[0]
    pairs = dates * per_date
    rows = phases.shape[0]
    chunk = 4
    fetches = [
        pltpu.make_async_copy(
            images_hbm.at[pl.ds(at, min(chunk, lines - at))],
            images.at[pl.ds(at, min(chunk, lines - at))],
            line_sem.at[at // chunk],
        )
        for at in range(0, lines, chunk)
    ]
    for fetch in fetches:
        fetch.start()
    loads = [
        pltpu.make_async_copy(weight_hbm.at[:, r], weights.at[r], load_sem.at[r])
        for r in range(rows)
    ]
    for load in loads:
        load.start()
    tile = lax.axis_index("tile")
    date = lax.axis_index("date")
    top = jnp.where(jnp.logical_and(tile == 0, date == 0), 0.0, 1.0)
    bottom = jnp.where(jnp.logical_and(tile == tiles - 1, date == 1), 0.0, 1.0)

    first = iota((pairs, 1), 0) // per_date
    first_pick = one_hot(iota((pairs, dates), 1) == first)
    of_date = lax.dot_general(
        first_pick,
        offsets[...].astype(F32).astype(BF16),
        (((1,), (1,)), ((), ())),
        preferred_element_type=F32,
    )
    own = iota((pairs, per_date), 1) == iota((pairs, per_date), 0) % per_date
    offset = jnp.sum(jnp.where(own, of_date, 0.0), axis=1, keepdims=True)
    second = first + offset.astype(jnp.int32)
    second_pick = one_hot(iota((pairs, dates), 1) == second)
    valid = jnp.where(second < dates, 1.0 / 255.0, 0.0)

    def form(at):
        image = images[at]
        a = mm(first_pick, image)
        b = mm(second_pick, image)
        a_re, a_im = a[:, :columns], a[:, columns:]
        b_re, b_im = b[:, :columns], b[:, columns:]
        formed[at, :, :columns] = a_re * b_re + a_im * b_im
        formed[at, :, columns:] = a_im * b_re - a_re * b_im

    for at in range(lines):
        if at % chunk == 0:
            fetches[at // chunk].wait()
        form(at)

    block_pairs = 8

    def build(block, carry):
        stencil_block(block, block_pairs, formed, coefs, top, bottom, half)
        return carry

    def unwrap(block, carry):
        sweep_block(block, block_pairs, lines, coefs, phases, half)
        return carry

    lax.fori_loop(0, pairs // block_pairs, build, 0)
    lax.fori_loop(0, pairs // block_pairs, unwrap, 0)

    for load in loads:
        load.wait()

    unknown = iota((pairs, dates), 1)
    covers = (unknown >= first) & (unknown < second) & (unknown < dates - 1)
    design = one_hot(covers)
    unknown_t = iota((dates, pairs), 0)
    first_t = iota((dates, pairs), 1) // per_date
    eye = iota((pairs, pairs), 0) == iota((pairs, pairs), 1)
    second_t = jnp.sum(jnp.where(eye, second.astype(F32), 0.0), axis=0, keepdims=True)
    covers_t = (unknown_t >= first_t) & (unknown_t < second_t.astype(jnp.int32))
    design_t = one_hot(covers_t & (unknown_t < dates - 1))
    design2 = jnp.concatenate([design, design], axis=1)
    design2_t = jnp.concatenate([design_t, design_t], axis=1)
    order = evens_first(columns)
    restore = one_hot(
        iota((columns, columns), 0)
        == (iota((columns, columns), 1) // 2 + (iota((columns, columns), 1) % 2) * half)
    )

    def forward(v):
        return mm(design2, jnp.concatenate(split(v), axis=0))

    def backward(x):
        return mm(design2_t, jnp.concatenate(split(x), axis=0))

    group = 8 if rows % 8 == 0 else 1

    def invert(at, carry):
        lanes = range(group)
        index = [at * group + g for g in lanes]
        y = [phases[i] for i in index]
        base = [mm(weights[i].astype(F32).astype(BF16), order) * valid for i in index]
        v = [None] * group
        for pass_index in range(PASSES):
            left = [y[g] - forward(v[g]) if pass_index else y[g] for g in lanes]
            w = [
                base[g] * rcp(1.0 + left[g] * left[g] * (1.0 / residual_scale**2))
                for g in lanes
            ]
            scale = [
                (1.0 / SPAN) * rcp(backward(w[g]) + solve_damping) for g in lanes
            ]
            for step_index in range(STEPS):
                if step_index:
                    left = [y[g] - forward(v[g]) for g in lanes]
                gradient = [backward(w[g] * left[g]) for g in lanes]
                for g in lanes:
                    if v[g] is None:
                        v[g] = gradient[g] * scale[g]
                    else:
                        v[g] = v[g] + (gradient[g] - solve_damping * v[g]) * scale[g]
        for g in lanes:
            high, rest = split(v[g])
            middle, low = split(v[g] - high.astype(F32))
            full = mm(high, restore) + (mm(middle, restore) + mm(low, restore))
            result[index[g]] = full[: dates - 1]
            save(index[g]).start()
        return carry

    def save(r):
        return pltpu.make_async_copy(result.at[r], out_hbm.at[:, r], save_sem.at[r])

    lax.fori_loop(0, rows // group, invert, 0)
    for r in range(rows):
        save(r).wait()


def solve(images, pair_offset, pair_weight, tiles):
    lines, dates, double = images.shape
    columns = double // 2
    pairs, rows = pair_weight.shape[:2]
    whole = pl.BlockSpec(memory_space=pltpu.VMEM)
    return pl.pallas_call(
        functools.partial(solve_kernel, tiles),
        out_shape=jax.ShapeDtypeStruct((dates - 1, rows, columns), F32),
        in_specs=[pl.BlockSpec(memory_space=pl.ANY), whole, pl.BlockSpec(memory_space=pl.ANY)],
        out_specs=pl.BlockSpec(memory_space=pl.ANY),
        scratch_shapes=[
            pltpu.VMEM(images.shape, BF16),
            pltpu.VMEM((lines, pairs, double), F32),
            pltpu.VMEM((lines, 10, pairs, columns // 2), F32),
            pltpu.VMEM((rows, pairs, columns), F32),
            pltpu.VMEM((rows, pairs, columns), jnp.int32),
            pltpu.VMEM((rows, dates - 1, columns), F32),
            pltpu.SemaphoreType.DMA((lines,)),
            pltpu.SemaphoreType.DMA((rows,)),
            pltpu.SemaphoreType.DMA((rows,)),
        ],
        compiler_params=pltpu.CompilerParams(vmem_limit_bytes=(64 << 20) - 1280 * 1024),
    )(images, pair_offset, pair_weight)


def local(slc_real, slc_imag, pair_offset, pair_weight, tiles):
    images = exchange(slc_real, slc_imag, tiles)
    return solve(images, pair_offset.T, pair_weight, tiles)


def solution(mesh):
    placed = (
        P("date", ("scene", "tile"), None),
        P("date", ("scene", "tile"), None),
        P(),
        P(None, ("scene", "tile", "date"), None),
    )
    return jax.shard_map(
        functools.partial(local, tiles=mesh.shape["tile"]),
        mesh=mesh,
        in_specs=placed,
        out_specs=P(None, ("scene", "tile", "date"), None),
        check_vma=False,
    )
```

```python
import functools

import jax
import jax.numpy as jnp
from jax import lax
from jax.experimental import pallas as pl
from jax.experimental.pallas import tpu as pltpu
from jax.sharding import PartitionSpec as P

SPAN = 5
SWEEPS = 8
PASSES = 3
STEPS = 2

unwrap_damping = 0.08
column_weight = 0.15
solve_damping = 0.1
residual_scale = 0.3

RIM = SWEEPS + 1
MESH = pl.DeviceIdType.MESH
F32 = jnp.float32
BF16 = jnp.bfloat16


def iota(shape, dim):
    return lax.broadcasted_iota(jnp.int32, shape, dim)


def one_hot(condition):
    return jnp.where(condition, 1.0, 0.0).astype(BF16)


def mm(a, b):
    return jnp.dot(a, b, preferred_element_type=F32)


def rcp(x):
    return pl.reciprocal(x, approx=True)


def split(x):
    high = x.astype(BF16)
    return high, (x - high.astype(F32)).astype(BF16)


def evens_first(columns):
    half = columns // 2
    new = iota((columns, columns), 1)
    old = jnp.where(new < half, 2 * new, 2 * (new - half) + 1)
    return one_hot(iota((columns, columns), 0) == old)


def exchange_kernel(
    tiles, re_hbm, im_hbm, out_ref, parts_ref, send_ref, zeros, load_sem, send_sem, recv_sem
):
    dates, tile_rows, columns = re_hbm.shape
    loads = [
        pltpu.make_async_copy(hbm, parts_ref.at[part], load_sem.at[part])
        for part, hbm in enumerate((re_hbm, im_hbm))
    ]
    for load in loads:
        load.start()
    shard = tile_rows // 2
    scene = lax.axis_index("scene")
    tile = lax.axis_index("tile")
    date = lax.axis_index("date")
    other = 1 - date
    has_up = tile > 0
    has_down = tile < tiles - 1
    barrier = pltpu.get_barrier_semaphore()

    def signal(to_tile, to_date):
        pl.semaphore_signal(
            barrier, inc=1, device_id=(scene, to_tile, to_date), device_id_type=MESH
        )

    signal(tile, other)

    @pl.when(jnp.logical_and(has_up, date == 0))
    def _():
        signal(tile - 1, 0)
        signal(tile - 1, 1)

    @pl.when(jnp.logical_and(has_down, date == 1))
    def _():
        signal(tile + 1, 0)
        signal(tile + 1, 1)

    order = evens_first(columns)
    count = dates * tile_rows

    def arrange(start, size):
        new = iota((size * dates, 1), 0) + start * dates
        old = (new % dates) * tile_rows + new // dates
        pick = one_hot(iota((size * dates, count), 1) == old)
        for part in range(2):
            moved = mm(pick, parts_ref[part].reshape(count, columns)).astype(BF16)
            send_ref[start : start + size, :, part * columns : (part + 1) * columns] = (
                mm(moved, order).astype(BF16).reshape(size, dates, columns)
            )

    for load in loads:
        load.wait()
    arrange(0, RIM)
    arrange(tile_rows - RIM, RIM)

    pl.semaphore_wait(barrier, 1 + has_up.astype(jnp.int32) + has_down.astype(jnp.int32))

    span = shard + RIM
    mine = pl.ds(pl.multiple_of(date * dates, dates), dates)

    def copy(source, target, to_tile, to_date, send_at, recv_at):
        return pltpu.make_async_remote_copy(
            src_ref=send_ref.at[source],
            dst_ref=out_ref.at[target, mine],
            send_sem=send_sem.at[send_at],
            recv_sem=recv_sem.at[recv_at],
            device_id=(scene, to_tile, to_date),
            device_id_type=MESH,
        )

    up_copy = copy(pl.ds(0, RIM), pl.ds(span, RIM), tile - 1, 1, 0, 1 + date)
    down_copy = copy(
        pl.ds(tile_rows - RIM, RIM), pl.ds(0, RIM), tile + 1, 0, 1, 1 + date
    )
    across = copy(
        pl.ds(other * (tile_rows - span), span),
        pl.ds(date * RIM, span),
        tile,
        other,
        2,
        0,
    )

    @pl.when(has_up)
    def _():
        up_copy.start()

    @pl.when(has_down)
    def _():
        down_copy.start()

    arrange(RIM, tile_rows - 2 * RIM)
    across.start()

    keep = pltpu.make_async_copy(
        send_ref.at[pl.ds(date * (tile_rows - span), span)],
        out_ref.at[pl.ds((1 - date) * RIM, span), mine],
        load_sem.at[0],
    )
    keep.start()
    missing = jnp.logical_or(
        jnp.logical_and(date == 0, tile == 0),
        jnp.logical_and(date == 1, tile == tiles - 1),
    )

    @pl.when(missing)
    def _():
        zeros[...] = jnp.zeros(zeros.shape, BF16)
        clear = pltpu.make_async_copy(
            zeros, out_ref.at[pl.ds(date * span, RIM)], load_sem.at[1]
        )
        clear.start()
        clear.wait()

    keep.wait()
    across.wait_send()

    @pl.when(has_up)
    def _():
        up_copy.wait_send()

    @pl.when(has_down)
    def _():
        down_copy.wait_send()

    across.wait_recv()

    @pl.when(jnp.logical_not(missing))
    def _():
        for sender in range(2):
            pltpu.make_async_remote_copy(
                src_ref=send_ref.at[pl.ds(0, RIM)],
                dst_ref=out_ref.at[pl.ds(0, RIM), mine],
                send_sem=send_sem.at[0],
                recv_sem=recv_sem.at[1 + sender],
                device_id=(scene, tile, other),
                device_id_type=MESH,
            ).wait_recv()


def exchange(slc_real, slc_imag, tiles):
    dates, tile_rows, columns = slc_real.shape
    shape = (tile_rows // 2 + 2 * RIM, 2 * dates, 2 * columns)
    return pl.pallas_call(
        functools.partial(exchange_kernel, tiles),
        out_shape=jax.ShapeDtypeStruct(shape, BF16),
        in_specs=[pl.BlockSpec(memory_space=pl.ANY)] * 2,
        out_specs=pl.BlockSpec(memory_space=pl.ANY),
        scratch_shapes=[
            pltpu.VMEM((2, dates, tile_rows, columns), BF16),
            pltpu.VMEM((tile_rows, dates, 2 * columns), BF16),
            pltpu.VMEM((RIM, 2 * dates, 2 * columns), BF16),
            pltpu.SemaphoreType.DMA((2,)),
            pltpu.SemaphoreType.DMA((3,)),
            pltpu.SemaphoreType.DMA((3,)),
        ],
        compiler_params=pltpu.CompilerParams(
            collective_id=0, has_side_effects=True, vmem_limit_bytes=(64 << 20) - 1280 * 1024
        ),
    )(slc_real, slc_imag)


def unwrap_block(block, pairs, formed, coefs, phases, top, bottom, half):
    lines = formed.shape[0]
    here = pl.ds(pl.multiple_of(block * pairs, pairs), pairs)
    lane = iota((pairs, half), 1)
    not_first = jnp.where(lane > 0, 1.0, 0.0)
    not_last = jnp.where(lane < half - 1, 1.0, 0.0)
    between = not_first * column_weight
    back = lambda x: pltpu.roll(x, 1, 1)
    ahead = lambda x: pltpu.roll(x, half - 1, 1)

    def line(at):
        return [formed[at, here, part * half : (part + 1) * half] for part in range(4)]

    smooth = {}
    upper = {}
    roots = {}
    levels = [dict() for _ in range(SWEEPS + 1)]

    def smooth_line(at, rows):
        result = []
        for part in (0, 2):
            even, odd = [rows[0][j] + rows[1][j] + rows[2][j] for j in (part, part + 1)]
            both = even + odd
            left = both + back(odd) * not_first
            right = both + ahead(even) * not_last
            if at == RIM - 1:
                left, right = left * top, right * top
            if at == lines - RIM:
                left, right = left * bottom, right * bottom
            result += [left, right]
        re_e, re_o, im_e, im_o = result
        size = []
        for re, im in ((re_e, im_e), (re_o, im_o)):
            power = re * re + im * im
            size.append(power * lax.rsqrt(jnp.maximum(power, 1e-30)))
        return (re_e, im_e, size[0]), (re_o, im_o, size[1])

    def couple(here_z, there_z, weight):
        product = here_z[2] * there_z[2]
        r = rcp(product + 81.0)
        link = product * r
        if weight is not None:
            link = link * weight
        cross = here_z[1] * there_z[0] - here_z[0] * there_z[1]
        return link, link * r * cross

    def stencil(at):
        even, odd = smooth[at]
        inner, inner_s = couple(even, odd, column_weight)
        outer, outer_s = couple(even, tuple(back(x) for x in odd), between)
        outer_next, outer_next_s = ahead(outer), ahead(outer_s)
        sides = ((outer, inner, outer_s + inner_s), (inner, outer_next, -inner_s - outer_next_s))
        root = []
        source = []
        for j in range(2):
            up, up_s = upper[at][j]
            down, down_s = upper[at + 1][j]
            left, right, side_s = sides[j]
            root.append(lax.rsqrt(up + down + left + right + unwrap_damping))
            source.append((up_s - down_s + side_s) * root[j])
            if at - 1 in roots:
                coefs[at, j] = up * (root[j] * roots[at - 1][j])
            coefs[at, 4 + j] = source[j]
            if RIM <= at < lines - RIM:
                coefs[at, 6 + j] = root[j]
        coefs[at, 2] = inner * (root[0] * root[1])
        coefs[at, 3] = outer * (root[0] * back(root[1]))
        roots[at] = root
        return source

    def sweep(at, values):
        above, below = values[at - 1], values[at + 1]
        even, odd = values[at]
        inner, outer = coefs[at, 2], coefs[at, 3]
        beside = (inner * odd + outer * back(odd), inner * even + ahead(outer * even))
        result = []
        for j in range(2):
            vertical = coefs[at, j] * above[j] + coefs[at + 1, j] * below[j]
            result.append((coefs[at, 4 + j] + vertical) + beside[j])
        return result

    window = [line(0), line(1)]
    for step in range(1, lines + SWEEPS):
        for level in range(SWEEPS, 1, -1):
            row = step - 1 - 2 * level
            if 1 + level <= row <= lines - 2 - level:
                values = sweep(row, levels[level - 1])
                levels[level][row] = values
                if level == SWEEPS:
                    for j in range(2):
                        phases[row - RIM, here, j * half : (j + 1) * half] = (
                            values[j] * coefs[row, 6 + j]
                        )
        if 2 <= step - 3 <= lines - 3:
            levels[1][step - 3] = stencil(step - 3)
        if 2 <= step - 1 <= lines - 2:
            upper[step - 1] = [
                couple(smooth[step - 1][j], smooth[step - 2][j], None) for j in range(2)
            ]
        if step <= lines - 2:
            window.append(line(step + 1))
            smooth[step] = smooth_line(step, window)
            window.pop(0)


def solve_kernel(
    tiles, images_hbm, offsets, weight_hbm, out_hbm, images, formed, coefs, phases, weights, result, line_sem, load_sem, save_sem
):
    lines, dates, double = images_hbm.shape
    columns = double // 2
    half = columns // 2
    per_date = offsets.shape[0]
    pairs = dates * per_date
    rows = phases.shape[0]
    chunk = 4
    fetches = [
        pltpu.make_async_copy(
            images_hbm.at[pl.ds(at, min(chunk, lines - at))],
            images.at[pl.ds(at, min(chunk, lines - at))],
            line_sem.at[at // chunk],
        )
        for at in range(0, lines, chunk)
    ]
    for fetch in fetches:
        fetch.start()
    loads = [
        pltpu.make_async_copy(weight_hbm.at[:, r], weights.at[r], load_sem.at[r])
        for r in range(rows)
    ]
    for load in loads:
        load.start()
    tile = lax.axis_index("tile")
    date = lax.axis_index("date")
    top = jnp.where(jnp.logical_and(tile == 0, date == 0), 0.0, 1.0)
    bottom = jnp.where(jnp.logical_and(tile == tiles - 1, date == 1), 0.0, 1.0)

    first = iota((pairs, 1), 0) // per_date
    first_pick = one_hot(iota((pairs, dates), 1) == first)
    of_date = lax.dot_general(
        first_pick,
        offsets[...].astype(F32).astype(BF16),
        (((1,), (1,)), ((), ())),
        preferred_element_type=F32,
    )
    own = iota((pairs, per_date), 1) == iota((pairs, per_date), 0) % per_date
    offset = jnp.sum(jnp.where(own, of_date, 0.0), axis=1, keepdims=True)
    second = first + offset.astype(jnp.int32)
    second_pick = one_hot(iota((pairs, dates), 1) == second)
    valid = jnp.where(second < dates, 1.0 / 255.0, 0.0)

    def form(at):
        image = images[at]
        a = mm(first_pick, image)
        b = mm(second_pick, image)
        a_re, a_im = a[:, :columns], a[:, columns:]
        b_re, b_im = b[:, :columns], b[:, columns:]
        formed[at, :, :columns] = a_re * b_re + a_im * b_im
        formed[at, :, columns:] = a_im * b_re - a_re * b_im

    for at in range(lines):
        if at % chunk == 0:
            fetches[at // chunk].wait()
        form(at)

    block_pairs = 8

    def unwrap(block, carry):
        unwrap_block(block, block_pairs, formed, coefs, phases, top, bottom, half)
        return carry

    lax.fori_loop(0, pairs // block_pairs, unwrap, 0)

    for load in loads:
        load.wait()

    unknown = iota((pairs, dates), 1)
    covers = (unknown >= first) & (unknown < second) & (unknown < dates - 1)
    design = one_hot(covers)
    unknown_t = iota((dates, pairs), 0)
    first_t = iota((dates, pairs), 1) // per_date
    eye = iota((pairs, pairs), 0) == iota((pairs, pairs), 1)
    second_t = jnp.sum(jnp.where(eye, second.astype(F32), 0.0), axis=0, keepdims=True)
    covers_t = (unknown_t >= first_t) & (unknown_t < second_t.astype(jnp.int32))
    design_t = one_hot(covers_t & (unknown_t < dates - 1))
    design2 = jnp.concatenate([design, design], axis=1)
    design2_t = jnp.concatenate([design_t, design_t], axis=1)
    order = evens_first(columns)
    restore = one_hot(
        iota((columns, columns), 0)
        == (iota((columns, columns), 1) // 2 + (iota((columns, columns), 1) % 2) * half)
    )

    def forward(v):
        return mm(design2, jnp.concatenate(split(v), axis=0))

    def backward(x):
        return mm(design2_t, jnp.concatenate(split(x), axis=0))

    group = 8 if rows % 8 == 0 else 1

    def invert(at, carry):
        lanes = range(group)
        index = [at * group + g for g in lanes]
        y = [phases[i] for i in index]
        base = [mm(weights[i].astype(F32).astype(BF16), order) * valid for i in index]
        v = [None] * group
        for pass_index in range(PASSES):
            left = [y[g] - forward(v[g]) if pass_index else y[g] for g in lanes]
            w = [
                base[g] * rcp(1.0 + left[g] * left[g] * (1.0 / residual_scale**2))
                for g in lanes
            ]
            scale = [
                (1.0 / SPAN) * rcp(backward(w[g]) + solve_damping) for g in lanes
            ]
            for step_index in range(STEPS):
                if step_index:
                    left = [y[g] - forward(v[g]) for g in lanes]
                gradient = [backward(w[g] * left[g]) for g in lanes]
                for g in lanes:
                    if v[g] is None:
                        v[g] = gradient[g] * scale[g]
                    else:
                        v[g] = v[g] + (gradient[g] - solve_damping * v[g]) * scale[g]
        for g in lanes:
            high, rest = split(v[g])
            middle, low = split(v[g] - high.astype(F32))
            full = mm(high, restore) + (mm(middle, restore) + mm(low, restore))
            result[index[g]] = full[: dates - 1]
            save(index[g]).start()
        return carry

    def save(r):
        return pltpu.make_async_copy(result.at[r], out_hbm.at[:, r], save_sem.at[r])

    lax.fori_loop(0, rows // group, invert, 0)
    for r in range(rows):
        save(r).wait()


def solve(images, pair_offset, pair_weight, tiles):
    lines, dates, double = images.shape
    columns = double // 2
    pairs, rows = pair_weight.shape[:2]
    whole = pl.BlockSpec(memory_space=pltpu.VMEM)
    return pl.pallas_call(
        functools.partial(solve_kernel, tiles),
        out_shape=jax.ShapeDtypeStruct((dates - 1, rows, columns), F32),
        in_specs=[pl.BlockSpec(memory_space=pl.ANY), whole, pl.BlockSpec(memory_space=pl.ANY)],
        out_specs=pl.BlockSpec(memory_space=pl.ANY),
        scratch_shapes=[
            pltpu.VMEM(images.shape, BF16),
            pltpu.VMEM((lines, pairs, double), F32),
            pltpu.VMEM((lines, 8, 8, columns // 2), F32),
            pltpu.VMEM((rows, pairs, columns), F32),
            pltpu.VMEM((rows, pairs, columns), jnp.int32),
            pltpu.VMEM((rows, dates - 1, columns), F32),
            pltpu.SemaphoreType.DMA((lines,)),
            pltpu.SemaphoreType.DMA((rows,)),
            pltpu.SemaphoreType.DMA((rows,)),
        ],
        compiler_params=pltpu.CompilerParams(vmem_limit_bytes=(64 << 20) - 1280 * 1024),
    )(images, pair_offset, pair_weight)


def local(slc_real, slc_imag, pair_offset, pair_weight, tiles):
    images = exchange(slc_real, slc_imag, tiles)
    return solve(images, pair_offset.T, pair_weight, tiles)


def solution(mesh):
    placed = (
        P("date", ("scene", "tile"), None),
        P("date", ("scene", "tile"), None),
        P(),
        P(None, ("scene", "tile", "date"), None),
    )
    return jax.shard_map(
        functools.partial(local, tiles=mesh.shape["tile"]),
        mesh=mesh,
        in_specs=placed,
        out_specs=P(None, ("scene", "tile", "date"), None),
        check_vma=False,
    )
```

```python
import functools

import jax
import jax.numpy as jnp
from jax import lax
from jax.experimental import pallas as pl
from jax.experimental.pallas import tpu as pltpu
from jax.sharding import PartitionSpec as P

SPAN = 5
SWEEPS = 8
PASSES = 3
STEPS = 2

unwrap_damping = 0.08
column_weight = 0.15
solve_damping = 0.1
residual_scale = 0.3

RIM = SWEEPS + 1
MESH = pl.DeviceIdType.MESH
F32 = jnp.float32
BF16 = jnp.bfloat16


def iota(shape, dim):
    return lax.broadcasted_iota(jnp.int32, shape, dim)


def one_hot(condition):
    return jnp.where(condition, 1.0, 0.0).astype(BF16)


def mm(a, b):
    return jnp.dot(a, b, preferred_element_type=F32)


def rcp(x):
    return pl.reciprocal(x, approx=True)


def split(x):
    high = x.astype(BF16)
    return high, (x - high.astype(F32)).astype(BF16)


def evens_first(columns):
    half = columns // 2
    new = iota((columns, columns), 1)
    old = jnp.where(new < half, 2 * new, 2 * (new - half) + 1)
    return one_hot(iota((columns, columns), 0) == old)


def exchange_kernel(
    tiles, re_hbm, im_hbm, out_ref, parts_ref, send_ref, zeros, load_sem, send_sem, recv_sem
):
    dates, tile_rows, columns = re_hbm.shape
    loads = [
        pltpu.make_async_copy(hbm, parts_ref.at[part], load_sem.at[part])
        for part, hbm in enumerate((re_hbm, im_hbm))
    ]
    for load in loads:
        load.start()
    shard = tile_rows // 2
    scene = lax.axis_index("scene")
    tile = lax.axis_index("tile")
    date = lax.axis_index("date")
    other = 1 - date
    has_up = tile > 0
    has_down = tile < tiles - 1
    barrier = pltpu.get_barrier_semaphore()

    def signal(to_tile, to_date):
        pl.semaphore_signal(
            barrier, inc=1, device_id=(scene, to_tile, to_date), device_id_type=MESH
        )

    signal(tile, other)

    @pl.when(jnp.logical_and(has_up, date == 0))
    def _():
        signal(tile - 1, 0)
        signal(tile - 1, 1)

    @pl.when(jnp.logical_and(has_down, date == 1))
    def _():
        signal(tile + 1, 0)
        signal(tile + 1, 1)

    order = evens_first(columns)
    count = dates * tile_rows

    def arrange(start, size):
        new = iota((size * dates, 1), 0) + start * dates
        old = (new % dates) * tile_rows + new // dates
        pick = one_hot(iota((size * dates, count), 1) == old)
        for part in range(2):
            moved = mm(pick, parts_ref[part].reshape(count, columns)).astype(BF16)
            send_ref[start : start + size, :, part * columns : (part + 1) * columns] = (
                mm(moved, order).astype(BF16).reshape(size, dates, columns)
            )

    for load in loads:
        load.wait()
    arrange(0, RIM)
    arrange(tile_rows - RIM, RIM)

    pl.semaphore_wait(barrier, 1 + has_up.astype(jnp.int32) + has_down.astype(jnp.int32))

    span = shard + RIM
    mine = pl.ds(pl.multiple_of(date * dates, dates), dates)

    def copy(source, target, to_tile, to_date, send_at, recv_at):
        return pltpu.make_async_remote_copy(
            src_ref=send_ref.at[source],
            dst_ref=out_ref.at[target, mine],
            send_sem=send_sem.at[send_at],
            recv_sem=recv_sem.at[recv_at],
            device_id=(scene, to_tile, to_date),
            device_id_type=MESH,
        )

    up_copy = copy(pl.ds(0, RIM), pl.ds(span, RIM), tile - 1, 1, 0, 1 + date)
    down_copy = copy(
        pl.ds(tile_rows - RIM, RIM), pl.ds(0, RIM), tile + 1, 0, 1, 1 + date
    )
    across = copy(
        pl.ds(other * (tile_rows - span), span),
        pl.ds(date * RIM, span),
        tile,
        other,
        2,
        0,
    )

    @pl.when(has_up)
    def _():
        up_copy.start()

    @pl.when(has_down)
    def _():
        down_copy.start()

    arrange(RIM, tile_rows - 2 * RIM)
    across.start()

    keep = pltpu.make_async_copy(
        send_ref.at[pl.ds(date * (tile_rows - span), span)],
        out_ref.at[pl.ds((1 - date) * RIM, span), mine],
        load_sem.at[0],
    )
    keep.start()
    missing = jnp.logical_or(
        jnp.logical_and(date == 0, tile == 0),
        jnp.logical_and(date == 1, tile == tiles - 1),
    )

    @pl.when(missing)
    def _():
        zeros[...] = jnp.zeros(zeros.shape, BF16)
        clear = pltpu.make_async_copy(
            zeros, out_ref.at[pl.ds(date * span, RIM)], load_sem.at[1]
        )
        clear.start()
        clear.wait()

    keep.wait()
    across.wait_send()

    @pl.when(has_up)
    def _():
        up_copy.wait_send()

    @pl.when(has_down)
    def _():
        down_copy.wait_send()

    across.wait_recv()

    @pl.when(jnp.logical_not(missing))
    def _():
        for sender in range(2):
            pltpu.make_async_remote_copy(
                src_ref=send_ref.at[pl.ds(0, RIM)],
                dst_ref=out_ref.at[pl.ds(0, RIM), mine],
                send_sem=send_sem.at[0],
                recv_sem=recv_sem.at[1 + sender],
                device_id=(scene, tile, other),
                device_id_type=MESH,
            ).wait_recv()


def exchange(slc_real, slc_imag, tiles):
    dates, tile_rows, columns = slc_real.shape
    shape = (tile_rows // 2 + 2 * RIM, 2 * dates, 2 * columns)
    return pl.pallas_call(
        functools.partial(exchange_kernel, tiles),
        out_shape=jax.ShapeDtypeStruct(shape, BF16),
        in_specs=[pl.BlockSpec(memory_space=pl.ANY)] * 2,
        out_specs=pl.BlockSpec(memory_space=pl.ANY),
        scratch_shapes=[
            pltpu.VMEM((2, dates, tile_rows, columns), BF16),
            pltpu.VMEM((tile_rows, dates, 2 * columns), BF16),
            pltpu.VMEM((RIM, 2 * dates, 2 * columns), BF16),
            pltpu.SemaphoreType.DMA((2,)),
            pltpu.SemaphoreType.DMA((3,)),
            pltpu.SemaphoreType.DMA((3,)),
        ],
        compiler_params=pltpu.CompilerParams(
            collective_id=0, has_side_effects=True, vmem_limit_bytes=(64 << 20) - 1280 * 1024
        ),
    )(slc_real, slc_imag)


def unwrap_block(block, pairs, formed, coefs, phases, top, bottom, half):
    lines = formed.shape[0]
    here = pl.ds(pl.multiple_of(block * pairs, pairs), pairs)
    lane = iota((pairs, half), 1)
    not_first = jnp.where(lane > 0, 1.0, 0.0)
    not_last = jnp.where(lane < half - 1, 1.0, 0.0)
    between = not_first * column_weight
    back = lambda x: pltpu.roll(x, 1, 1)
    ahead = lambda x: pltpu.roll(x, half - 1, 1)

    def line(at):
        return [formed[at, here, part * half : (part + 1) * half] for part in range(4)]

    smooth = {}
    upper = {}
    roots = {}
    levels = [dict() for _ in range(SWEEPS + 1)]

    def smooth_line(at, rows):
        result = []
        for part in (0, 2):
            even, odd = [rows[0][j] + rows[1][j] + rows[2][j] for j in (part, part + 1)]
            both = even + odd
            left = both + back(odd) * not_first
            right = both + ahead(even) * not_last
            if at == RIM - 1:
                left, right = left * top, right * top
            if at == lines - RIM:
                left, right = left * bottom, right * bottom
            result += [left, right]
        re_e, re_o, im_e, im_o = result
        size = []
        for re, im in ((re_e, im_e), (re_o, im_o)):
            power = re * re + im * im
            size.append(power * lax.rsqrt(jnp.maximum(power, 1e-30)))
        return (re_e, im_e, size[0]), (re_o, im_o, size[1])

    def couple(here_z, there_z, weight):
        product = here_z[2] * there_z[2]
        r = rcp(product + 81.0)
        link = product * r
        if weight is not None:
            link = link * weight
        cross = here_z[1] * there_z[0] - here_z[0] * there_z[1]
        return link, link * r * cross

    def stencil(at):
        even, odd = smooth[at]
        inner, inner_s = couple(even, odd, column_weight)
        outer, outer_s = couple(even, tuple(back(x) for x in odd), between)
        outer_next, outer_next_s = ahead(outer), ahead(outer_s)
        sides = ((outer, inner, outer_s + inner_s), (inner, outer_next, -inner_s - outer_next_s))
        root = []
        source = []
        for j in range(2):
            up, up_s = upper[at][j]
            down, down_s = upper[at + 1][j]
            left, right, side_s = sides[j]
            root.append(lax.rsqrt(up + down + left + right + unwrap_damping))
            source.append((up_s - down_s + side_s) * root[j])
            if at - 1 in roots:
                coefs[at, j] = up * (root[j] * roots[at - 1][j])
            coefs[at, 4 + j] = source[j]
            if RIM <= at < lines - RIM:
                coefs[at, 6 + j] = root[j]
        coefs[at, 2] = inner * (root[0] * root[1])
        coefs[at, 3] = outer * (root[0] * back(root[1]))
        roots[at] = root
        return source

    def sweep(at, values):
        above, below = values[at - 1], values[at + 1]
        even, odd = values[at]
        inner, outer = coefs[at, 2], coefs[at, 3]
        beside = (inner * odd + outer * back(odd), inner * even + ahead(outer * even))
        result = []
        for j in range(2):
            vertical = coefs[at, j] * above[j] + coefs[at + 1, j] * below[j]
            result.append((coefs[at, 4 + j] + vertical) + beside[j])
        return result

    window = [line(0), line(1)]
    for step in range(1, lines + SWEEPS):
        for level in range(SWEEPS, 1, -1):
            row = step - 1 - 2 * level
            if 1 + level <= row <= lines - 2 - level:
                values = sweep(row, levels[level - 1])
                levels[level][row] = values
                if level == SWEEPS:
                    for j in range(2):
                        phases[row - RIM, here, j * half : (j + 1) * half] = (
                            values[j] * coefs[row, 6 + j]
                        )
        if 2 <= step - 3 <= lines - 3:
            levels[1][step - 3] = stencil(step - 3)
        if 2 <= step - 1 <= lines - 2:
            upper[step - 1] = [
                couple(smooth[step - 1][j], smooth[step - 2][j], None) for j in range(2)
            ]
        if step <= lines - 2:
            window.append(line(step + 1))
            smooth[step] = smooth_line(step, window)
            window.pop(0)


def solve_kernel(
    tiles, images_hbm, offsets, weight_hbm, out_hbm, images, formed, coefs, phases, weights, result, line_sem, load_sem, save_sem
):
    lines, dates, double = images_hbm.shape
    columns = double // 2
    half = columns // 2
    per_date = offsets.shape[0]
    pairs = dates * per_date
    rows = phases.shape[0]
    chunk = (lines + 1) // 2
    fetches = [
        pltpu.make_async_copy(
            images_hbm.at[pl.ds(at, min(chunk, lines - at))],
            images.at[pl.ds(at, min(chunk, lines - at))],
            line_sem.at[at // chunk],
        )
        for at in range(0, lines, chunk)
    ]
    for fetch in fetches:
        fetch.start()
    loads = [
        pltpu.make_async_copy(weight_hbm.at[:, r], weights.at[r], load_sem.at[r])
        for r in range(rows)
    ]
    for load in loads:
        load.start()
    tile = lax.axis_index("tile")
    date = lax.axis_index("date")
    top = jnp.where(jnp.logical_and(tile == 0, date == 0), 0.0, 1.0)
    bottom = jnp.where(jnp.logical_and(tile == tiles - 1, date == 1), 0.0, 1.0)

    first = iota((pairs, 1), 0) // per_date
    first_pick = one_hot(iota((pairs, dates), 1) == first)
    of_date = lax.dot_general(
        first_pick,
        offsets[...].astype(F32).astype(BF16),
        (((1,), (1,)), ((), ())),
        preferred_element_type=F32,
    )
    own = iota((pairs, per_date), 1) == iota((pairs, per_date), 0) % per_date
    offset = jnp.sum(jnp.where(own, of_date, 0.0), axis=1, keepdims=True)
    second = first + offset.astype(jnp.int32)
    second_pick = one_hot(iota((pairs, dates), 1) == second)
    valid = jnp.where(second < dates, 1.0 / 255.0, 0.0)

    def form(at):
        image = images[at]
        a = mm(first_pick, image)
        b = mm(second_pick, image)
        a_re, a_im = a[:, :columns], a[:, columns:]
        b_re, b_im = b[:, :columns], b[:, columns:]
        formed[at, :, :columns] = a_re * b_re + a_im * b_im
        formed[at, :, columns:] = a_im * b_re - a_re * b_im

    for at in range(lines):
        if at % chunk == 0:
            fetches[at // chunk].wait()
        form(at)

    block_pairs = 8

    def unwrap(block, carry):
        unwrap_block(block, block_pairs, formed, coefs, phases, top, bottom, half)
        return carry

    lax.fori_loop(0, pairs // block_pairs, unwrap, 0)

    for load in loads:
        load.wait()

    unknown = iota((pairs, dates), 1)
    covers = (unknown >= first) & (unknown < second) & (unknown < dates - 1)
    design = one_hot(covers)
    unknown_t = iota((dates, pairs), 0)
    first_t = iota((dates, pairs), 1) // per_date
    eye = iota((pairs, pairs), 0) == iota((pairs, pairs), 1)
    second_t = jnp.sum(jnp.where(eye, second.astype(F32), 0.0), axis=0, keepdims=True)
    covers_t = (unknown_t >= first_t) & (unknown_t < second_t.astype(jnp.int32))
    design_t = one_hot(covers_t & (unknown_t < dates - 1))
    design2 = jnp.concatenate([design, design], axis=1)
    design2_t = jnp.concatenate([design_t, design_t], axis=1)
    order = evens_first(columns)
    restore = one_hot(
        iota((columns, columns), 0)
        == (iota((columns, columns), 1) // 2 + (iota((columns, columns), 1) % 2) * half)
    )

    def forward(v):
        return mm(design2, jnp.concatenate(split(v), axis=0))

    def backward(x):
        return mm(design2_t, jnp.concatenate(split(x), axis=0))

    group = 8 if rows % 8 == 0 else 1

    def invert(at, carry):
        lanes = range(group)
        index = [at * group + g for g in lanes]
        y = [phases[i] for i in index]
        base = [mm(weights[i].astype(F32).astype(BF16), order) * valid for i in index]
        v = [None] * group
        for pass_index in range(PASSES):
            left = [y[g] - forward(v[g]) if pass_index else y[g] for g in lanes]
            w = [
                base[g] * rcp(1.0 + left[g] * left[g] * (1.0 / residual_scale**2))
                for g in lanes
            ]
            scale = [
                (1.0 / SPAN) * rcp(backward(w[g]) + solve_damping) for g in lanes
            ]
            for step_index in range(STEPS):
                if step_index:
                    left = [y[g] - forward(v[g]) for g in lanes]
                gradient = [backward(w[g] * left[g]) for g in lanes]
                for g in lanes:
                    if v[g] is None:
                        v[g] = gradient[g] * scale[g]
                    else:
                        v[g] = v[g] + (gradient[g] - solve_damping * v[g]) * scale[g]
        for g in lanes:
            high, rest = split(v[g])
            middle, low = split(v[g] - high.astype(F32))
            full = mm(high, restore) + (mm(middle, restore) + mm(low, restore))
            result[index[g]] = full[: dates - 1]
        return carry

    def save(r):
        return pltpu.make_async_copy(result.at[r], out_hbm.at[:, r], save_sem.at[r])

    lax.fori_loop(0, rows // group, invert, 0)
    for r in range(rows):
        save(r).start()
    for r in range(rows):
        save(r).wait()


def solve(images, pair_offset, pair_weight, tiles):
    lines, dates, double = images.shape
    columns = double // 2
    pairs, rows = pair_weight.shape[:2]
    whole = pl.BlockSpec(memory_space=pltpu.VMEM)
    return pl.pallas_call(
        functools.partial(solve_kernel, tiles),
        out_shape=jax.ShapeDtypeStruct((dates - 1, rows, columns), F32),
        in_specs=[pl.BlockSpec(memory_space=pl.ANY), whole, pl.BlockSpec(memory_space=pl.ANY)],
        out_specs=pl.BlockSpec(memory_space=pl.ANY),
        scratch_shapes=[
            pltpu.VMEM(images.shape, BF16),
            pltpu.VMEM((lines, pairs, double), F32),
            pltpu.VMEM((lines, 8, 8, columns // 2), F32),
            pltpu.VMEM((rows, pairs, columns), F32),
            pltpu.VMEM((rows, pairs, columns), jnp.int32),
            pltpu.VMEM((rows, dates - 1, columns), F32),
            pltpu.SemaphoreType.DMA((lines,)),
            pltpu.SemaphoreType.DMA((rows,)),
            pltpu.SemaphoreType.DMA((rows,)),
        ],
        compiler_params=pltpu.CompilerParams(vmem_limit_bytes=(64 << 20) - 1280 * 1024),
    )(images, pair_offset, pair_weight)


def local(slc_real, slc_imag, pair_offset, pair_weight, tiles):
    images = exchange(slc_real, slc_imag, tiles)
    return solve(images, pair_offset.T, pair_weight, tiles)


def solution(mesh):
    placed = (
        P("date", ("scene", "tile"), None),
        P("date", ("scene", "tile"), None),
        P(),
        P(None, ("scene", "tile", "date"), None),
    )
    return jax.shard_map(
        functools.partial(local, tiles=mesh.shape["tile"]),
        mesh=mesh,
        in_specs=placed,
        out_specs=P(None, ("scene", "tile", "date"), None),
        check_vma=False,
    )
```

```python
import functools

import jax
import jax.numpy as jnp
from jax import lax
from jax.experimental import pallas as pl
from jax.experimental.pallas import tpu as pltpu
from jax.sharding import PartitionSpec as P

SPAN = 5
SWEEPS = 8
PASSES = 3
STEPS = 2

unwrap_damping = 0.08
column_weight = 0.15
solve_damping = 0.1
residual_scale = 0.3

RIM = SWEEPS + 1
MESH = pl.DeviceIdType.MESH
F32 = jnp.float32
BF16 = jnp.bfloat16


def iota(shape, dim):
    return lax.broadcasted_iota(jnp.int32, shape, dim)


def one_hot(condition):
    return jnp.where(condition, 1.0, 0.0).astype(BF16)


def mm(a, b):
    return jnp.dot(a, b, preferred_element_type=F32)


def rcp(x):
    return pl.reciprocal(x, approx=True)


def split(x):
    high = x.astype(BF16)
    return high, (x - high.astype(F32)).astype(BF16)


def evens_first(columns):
    half = columns // 2
    new = iota((columns, columns), 1)
    old = jnp.where(new < half, 2 * new, 2 * (new - half) + 1)
    return one_hot(iota((columns, columns), 0) == old)


def exchange_kernel(
    tiles, re_hbm, im_hbm, out_ref, parts_ref, send_ref, zeros, load_sem, send_sem, recv_sem
):
    dates, tile_rows, columns = re_hbm.shape
    loads = [
        pltpu.make_async_copy(hbm, parts_ref.at[part], load_sem.at[part])
        for part, hbm in enumerate((re_hbm, im_hbm))
    ]
    for load in loads:
        load.start()
    shard = tile_rows // 2
    scene = lax.axis_index("scene")
    tile = lax.axis_index("tile")
    date = lax.axis_index("date")
    other = 1 - date
    has_up = tile > 0
    has_down = tile < tiles - 1
    barrier = pltpu.get_barrier_semaphore()

    def signal(to_tile, to_date):
        pl.semaphore_signal(
            barrier, inc=1, device_id=(scene, to_tile, to_date), device_id_type=MESH
        )

    signal(tile, other)

    @pl.when(jnp.logical_and(has_up, date == 0))
    def _():
        signal(tile - 1, 0)
        signal(tile - 1, 1)

    @pl.when(jnp.logical_and(has_down, date == 1))
    def _():
        signal(tile + 1, 0)
        signal(tile + 1, 1)

    order = evens_first(columns)
    count = dates * tile_rows

    def arrange(start, size):
        new = iota((size * dates, 1), 0) + start * dates
        old = (new % dates) * tile_rows + new // dates
        pick = one_hot(iota((size * dates, count), 1) == old)
        for part in range(2):
            moved = mm(pick, parts_ref[part].reshape(count, columns)).astype(BF16)
            send_ref[start : start + size, :, part * columns : (part + 1) * columns] = (
                mm(moved, order).astype(BF16).reshape(size, dates, columns)
            )

    for load in loads:
        load.wait()
    arrange(0, RIM)
    arrange(tile_rows - RIM, RIM)

    pl.semaphore_wait(barrier, 1 + has_up.astype(jnp.int32) + has_down.astype(jnp.int32))

    span = shard + RIM
    mine = pl.ds(pl.multiple_of(date * dates, dates), dates)

    def copy(source, target, to_tile, to_date, send_at, recv_at):
        return pltpu.make_async_remote_copy(
            src_ref=send_ref.at[source],
            dst_ref=out_ref.at[target, mine],
            send_sem=send_sem.at[send_at],
            recv_sem=recv_sem.at[recv_at],
            device_id=(scene, to_tile, to_date),
            device_id_type=MESH,
        )

    up_copy = copy(pl.ds(0, RIM), pl.ds(span, RIM), tile - 1, 1, 0, 1 + date)
    down_copy = copy(
        pl.ds(tile_rows - RIM, RIM), pl.ds(0, RIM), tile + 1, 0, 1, 1 + date
    )
    across = copy(
        pl.ds(other * (tile_rows - span), span),
        pl.ds(date * RIM, span),
        tile,
        other,
        2,
        0,
    )

    @pl.when(has_up)
    def _():
        up_copy.start()

    @pl.when(has_down)
    def _():
        down_copy.start()

    arrange(RIM, tile_rows - 2 * RIM)
    across.start()

    keep = pltpu.make_async_copy(
        send_ref.at[pl.ds(date * (tile_rows - span), span)],
        out_ref.at[pl.ds((1 - date) * RIM, span), mine],
        load_sem.at[0],
    )
    keep.start()
    missing = jnp.logical_or(
        jnp.logical_and(date == 0, tile == 0),
        jnp.logical_and(date == 1, tile == tiles - 1),
    )

    @pl.when(missing)
    def _():
        zeros[...] = jnp.zeros(zeros.shape, BF16)
        clear = pltpu.make_async_copy(
            zeros, out_ref.at[pl.ds(date * span, RIM)], load_sem.at[1]
        )
        clear.start()
        clear.wait()

    keep.wait()
    across.wait_send()

    @pl.when(has_up)
    def _():
        up_copy.wait_send()

    @pl.when(has_down)
    def _():
        down_copy.wait_send()

    across.wait_recv()

    @pl.when(jnp.logical_not(missing))
    def _():
        for sender in range(2):
            pltpu.make_async_remote_copy(
                src_ref=send_ref.at[pl.ds(0, RIM)],
                dst_ref=out_ref.at[pl.ds(0, RIM), mine],
                send_sem=send_sem.at[0],
                recv_sem=recv_sem.at[1 + sender],
                device_id=(scene, tile, other),
                device_id_type=MESH,
            ).wait_recv()


def exchange(slc_real, slc_imag, tiles):
    dates, tile_rows, columns = slc_real.shape
    shape = (tile_rows // 2 + 2 * RIM, 2 * dates, 2 * columns)
    return pl.pallas_call(
        functools.partial(exchange_kernel, tiles),
        out_shape=jax.ShapeDtypeStruct(shape, BF16),
        in_specs=[pl.BlockSpec(memory_space=pl.ANY)] * 2,
        out_specs=pl.BlockSpec(memory_space=pl.ANY),
        scratch_shapes=[
            pltpu.VMEM((2, dates, tile_rows, columns), BF16),
            pltpu.VMEM((tile_rows, dates, 2 * columns), BF16),
            pltpu.VMEM((RIM, 2 * dates, 2 * columns), BF16),
            pltpu.SemaphoreType.DMA((2,)),
            pltpu.SemaphoreType.DMA((3,)),
            pltpu.SemaphoreType.DMA((3,)),
        ],
        compiler_params=pltpu.CompilerParams(
            collective_id=0, has_side_effects=True, vmem_limit_bytes=(64 << 20) - 1280 * 1024
        ),
    )(slc_real, slc_imag)


def unwrap_block(block, pairs, formed, coefs, phases, top, bottom, half):
    lines = formed.shape[0]
    here = pl.ds(pl.multiple_of(block * pairs, pairs), pairs)
    lane = iota((pairs, half), 1)
    not_first = jnp.where(lane > 0, 1.0, 0.0)
    not_last = jnp.where(lane < half - 1, 1.0, 0.0)
    between = not_first * column_weight
    back = lambda x: pltpu.roll(x, 1, 1)
    ahead = lambda x: pltpu.roll(x, half - 1, 1)

    def line(at):
        return [formed[at, here, part * half : (part + 1) * half] for part in range(4)]

    smooth = {}
    upper = {}
    levels = [dict() for _ in range(SWEEPS + 1)]

    def smooth_line(at, rows):
        result = []
        for part in (0, 2):
            even, odd = [rows[0][j] + rows[1][j] + rows[2][j] for j in (part, part + 1)]
            both = even + odd
            left = both + back(odd) * not_first
            right = both + ahead(even) * not_last
            if at == RIM - 1:
                left, right = left * top, right * top
            if at == lines - RIM:
                left, right = left * bottom, right * bottom
            result += [left, right]
        re_e, re_o, im_e, im_o = result
        size = []
        for re, im in ((re_e, im_e), (re_o, im_o)):
            power = re * re + im * im
            size.append(power * lax.rsqrt(jnp.maximum(power, 1e-30)))
        return (re_e, im_e, size[0]), (re_o, im_o, size[1])

    def couple(here_z, there_z, weight):
        product = here_z[2] * there_z[2]
        r = rcp(product + 81.0)
        link = product * r
        if weight is not None:
            link = link * weight
        cross = here_z[1] * there_z[0] - here_z[0] * there_z[1]
        return link, link * r * cross

    def stencil(at):
        even, odd = smooth[at]
        inner, inner_s = couple(even, odd, column_weight)
        outer, outer_s = couple(even, tuple(back(x) for x in odd), between)
        outer_next, outer_next_s = ahead(outer), ahead(outer_s)
        sides = ((outer, inner, outer_s + inner_s), (inner, outer_next, -inner_s - outer_next_s))
        first = []
        for j in range(2):
            up, up_s = upper[at][j]
            down, down_s = upper[at + 1][j]
            left, right, side_s = sides[j]
            scale = rcp(up + down + left + right + unwrap_damping)
            source = (up_s - down_s + side_s) * scale
            for k, value in enumerate((up, down, left, right)):
                coefs[at, 5 * j + k] = value * scale
            coefs[at, 5 * j + 4] = source
            first.append(source)
        return first

    def sweep(at, values):
        above, below = values[at - 1], values[at + 1]
        even, odd = values[at]
        beside = ((back(odd), odd), (even, ahead(even)))
        result = []
        for j in range(2):
            vertical = coefs[at, 5 * j] * above[j] + coefs[at, 5 * j + 1] * below[j]
            sides = coefs[at, 5 * j + 2] * beside[j][0] + coefs[at, 5 * j + 3] * beside[j][1]
            total = (coefs[at, 5 * j + 4] + vertical) + sides
            result.append(total)
        return result

    window = [line(0), line(1)]
    for step in range(1, lines + SWEEPS):
        for level in range(SWEEPS, 1, -1):
            row = step - 1 - 2 * level
            if 1 + level <= row <= lines - 2 - level:
                values = sweep(row, levels[level - 1])
                levels[level][row] = values
                if level == SWEEPS:
                    for j in range(2):
                        phases[row - RIM, here, j * half : (j + 1) * half] = values[j]
        if 2 <= step - 3 <= lines - 3:
            levels[1][step - 3] = stencil(step - 3)
        if 2 <= step - 1 <= lines - 2:
            upper[step - 1] = [
                couple(smooth[step - 1][j], smooth[step - 2][j], None) for j in range(2)
            ]
        if step <= lines - 2:
            window.append(line(step + 1))
            smooth[step] = smooth_line(step, window)
            window.pop(0)


def solve_kernel(
    tiles, images_hbm, offsets, weight_hbm, out_hbm, images, formed, coefs, phases, weights, result, line_sem, load_sem, save_sem
):
    lines, dates, double = images_hbm.shape
    columns = double // 2
    half = columns // 2
    per_date = offsets.shape[0]
    pairs = dates * per_date
    rows = phases.shape[0]
    chunk = (lines + 1) // 2
    fetches = [
        pltpu.make_async_copy(
            images_hbm.at[pl.ds(at, min(chunk, lines - at))],
            images.at[pl.ds(at, min(chunk, lines - at))],
            line_sem.at[at // chunk],
        )
        for at in range(0, lines, chunk)
    ]
    for fetch in fetches:
        fetch.start()
    loads = [
        pltpu.make_async_copy(weight_hbm.at[:, r], weights.at[r], load_sem.at[r])
        for r in range(rows)
    ]
    for load in loads:
        load.start()
    tile = lax.axis_index("tile")
    date = lax.axis_index("date")
    top = jnp.where(jnp.logical_and(tile == 0, date == 0), 0.0, 1.0)
    bottom = jnp.where(jnp.logical_and(tile == tiles - 1, date == 1), 0.0, 1.0)

    first = iota((pairs, 1), 0) // per_date
    first_pick = one_hot(iota((pairs, dates), 1) == first)
    of_date = lax.dot_general(
        first_pick,
        offsets[...].astype(F32).astype(BF16),
        (((1,), (1,)), ((), ())),
        preferred_element_type=F32,
    )
    own = iota((pairs, per_date), 1) == iota((pairs, per_date), 0) % per_date
    offset = jnp.sum(jnp.where(own, of_date, 0.0), axis=1, keepdims=True)
    second = first + offset.astype(jnp.int32)
    second_pick = one_hot(iota((pairs, dates), 1) == second)
    valid = jnp.where(second < dates, 1.0 / 255.0, 0.0)

    def form(at):
        image = images[at]
        a = mm(first_pick, image)
        b = mm(second_pick, image)
        a_re, a_im = a[:, :columns], a[:, columns:]
        b_re, b_im = b[:, :columns], b[:, columns:]
        formed[at, :, :columns] = a_re * b_re + a_im * b_im
        formed[at, :, columns:] = a_im * b_re - a_re * b_im

    for at in range(lines):
        if at % chunk == 0:
            fetches[at // chunk].wait()
        form(at)

    block_pairs = 8

    def unwrap(block, carry):
        unwrap_block(block, block_pairs, formed, coefs, phases, top, bottom, half)
        return carry

    lax.fori_loop(0, pairs // block_pairs, unwrap, 0)

    for load in loads:
        load.wait()

    unknown = iota((pairs, dates), 1)
    covers = (unknown >= first) & (unknown < second) & (unknown < dates - 1)
    design = one_hot(covers)
    unknown_t = iota((dates, pairs), 0)
    first_t = iota((dates, pairs), 1) // per_date
    eye = iota((pairs, pairs), 0) == iota((pairs, pairs), 1)
    second_t = jnp.sum(jnp.where(eye, second.astype(F32), 0.0), axis=0, keepdims=True)
    covers_t = (unknown_t >= first_t) & (unknown_t < second_t.astype(jnp.int32))
    design_t = one_hot(covers_t & (unknown_t < dates - 1))
    design2 = jnp.concatenate([design, design], axis=1)
    design2_t = jnp.concatenate([design_t, design_t], axis=1)
    order = evens_first(columns)
    restore = one_hot(
        iota((columns, columns), 0)
        == (iota((columns, columns), 1) // 2 + (iota((columns, columns), 1) % 2) * half)
    )

    def forward(v):
        return mm(design2, jnp.concatenate(split(v), axis=0))

    def backward(x):
        return mm(design2_t, jnp.concatenate(split(x), axis=0))

    group = 16 if rows % 16 == 0 else 1

    def invert(at, carry):
        lanes = range(group)
        index = [at * group + g for g in lanes]
        y = [phases[i] for i in index]
        base = [mm(weights[i].astype(F32).astype(BF16), order) * valid for i in index]
        v = [None] * group
        for pass_index in range(PASSES):
            left = [y[g] - forward(v[g]) if pass_index else y[g] for g in lanes]
            w = [
                base[g] * rcp(1.0 + left[g] * left[g] * (1.0 / residual_scale**2))
                for g in lanes
            ]
            scale = [
                (1.0 / SPAN) * rcp(backward(w[g]) + solve_damping) for g in lanes
            ]
            for step_index in range(STEPS):
                if step_index:
                    left = [y[g] - forward(v[g]) for g in lanes]
                gradient = [backward(w[g] * left[g]) for g in lanes]
                for g in lanes:
                    if v[g] is None:
                        v[g] = gradient[g] * scale[g]
                    else:
                        v[g] = v[g] + (gradient[g] - solve_damping * v[g]) * scale[g]
        for g in lanes:
            high, rest = split(v[g])
            middle, low = split(v[g] - high.astype(F32))
            full = mm(high, restore) + (mm(middle, restore) + mm(low, restore))
            result[index[g]] = full[: dates - 1]
        return carry

    lax.fori_loop(0, rows // group, invert, 0)
    saves = [
        pltpu.make_async_copy(result.at[r], out_hbm.at[:, r], save_sem.at[r])
        for r in range(rows)
    ]
    for save in saves:
        save.start()
    for save in saves:
        save.wait()


def solve(images, pair_offset, pair_weight, tiles):
    lines, dates, double = images.shape
    columns = double // 2
    pairs, rows = pair_weight.shape[:2]
    whole = pl.BlockSpec(memory_space=pltpu.VMEM)
    return pl.pallas_call(
        functools.partial(solve_kernel, tiles),
        out_shape=jax.ShapeDtypeStruct((dates - 1, rows, columns), F32),
        in_specs=[pl.BlockSpec(memory_space=pl.ANY), whole, pl.BlockSpec(memory_space=pl.ANY)],
        out_specs=pl.BlockSpec(memory_space=pl.ANY),
        scratch_shapes=[
            pltpu.VMEM(images.shape, BF16),
            pltpu.VMEM((lines, pairs, double), F32),
            pltpu.VMEM((lines, 10, 8, columns // 2), F32),
            pltpu.VMEM((rows, pairs, columns), F32),
            pltpu.VMEM((rows, pairs, columns), jnp.int32),
            pltpu.VMEM((rows, dates - 1, columns), F32),
            pltpu.SemaphoreType.DMA((lines,)),
            pltpu.SemaphoreType.DMA((rows,)),
            pltpu.SemaphoreType.DMA((rows,)),
        ],
        compiler_params=pltpu.CompilerParams(vmem_limit_bytes=(64 << 20) - 1280 * 1024),
    )(images, pair_offset, pair_weight)


def local(slc_real, slc_imag, pair_offset, pair_weight, tiles):
    images = exchange(slc_real, slc_imag, tiles)
    return solve(images, pair_offset.T, pair_weight, tiles)


def solution(mesh):
    placed = (
        P("date", ("scene", "tile"), None),
        P("date", ("scene", "tile"), None),
        P(),
        P(None, ("scene", "tile", "date"), None),
    )
    return jax.shard_map(
        functools.partial(local, tiles=mesh.shape["tile"]),
        mesh=mesh,
        in_specs=placed,
        out_specs=P(None, ("scene", "tile", "date"), None),
        check_vma=False,
    )
```
